128 devices in a mesh: feat: 8 (over z, y_lo), tile: 16 (over y_hi, x, core).
Axes of the slice: x: 4, y: 4 (y_hi: 2, y_lo: 2; y = y_hi * 2 + y_lo), z: 4, core: 2. Of those that a mesh axis runs over, the one named last changes fastest.
Arguments:
- images: bfloat16 [12288, 12288], P(('feat', 'tile')), may hold values from -6 to 6
- row_list: int32 [12288], P(('feat', 'tile')), may hold values from 0 to 95
- labels: int32 [12288], P(('feat', 'tile')), may hold values from 0 to 999
- filters: bfloat16 [6, 6, 3, 1024], replicated, may hold values from -0.625 to 0.625
- bias: float32 [1024], replicated, may hold values from -0.8 to 0.4
- tile_owner: int32 [136], replicated, may hold values from 0 to 15, as said below
Outputs:
- gram_tiles: float32 [320, 256, 256], P('tile', 'feat')
- cross: float32 [4096, 1000], P(('feat', 'tile'))
The draws below stay inside these ranges and needn't reach their ends.
Inputs may be any that keep to these rules, and one draw needn't show every extreme that they name: `row_list`: each entry indexes the stored images of the device that holds that entry's position. `tile_owner`: no owner has more than 20 tiles, and one owner has exactly 20.
All inputs are finite; a program needn't handle non-finite values.
Results may differ from the reference program's by a relative error of at most 0.0003.
Values may be sent and summed in bfloat16 or wider, within the bound.
No kernel may reach another device: no remote copies, remote signals or barrier semaphores. Data moves between devices by JAX's collectives and lax.ppermute only.
A program may use at most 192 MiB of HBM per device.

```python
import jax
import jax.numpy as jnp
import numpy as np
from jax import lax

IMG = 64
FILTERS = 1024
D = 4096
TS = 256
NB = 16
NTILES = 136
MAXT = 20
CLASSES = 1000
ROWS_DEV = 96
IMAGES = 12288
N_TILE = 16


def draw_tile_owner(key, part):
    key = jax.random.fold_in(key, 7)
    tile_order = jax.random.permutation(jax.random.fold_in(key, 1), NTILES).astype(jnp.int32)
    owner_order = jax.random.permutation(jax.random.fold_in(key, 2), N_TILE).astype(jnp.int32)
    places = jnp.arange(NTILES, dtype=jnp.int32)
    others = owner_order[1 + jnp.mod(places - MAXT, N_TILE - 1)]
    chosen = jnp.where(places < MAXT, owner_order[0], others).astype(jnp.int32)
    return jnp.zeros((NTILES,), jnp.int32).at[tile_order].set(chosen)


def touch_ends(drawn, own_key, low, top_value):
    place = [jax.random.randint(jax.random.fold_in(own_key, axis), (), 0, length) for axis, length in enumerate(drawn.shape)]
    main_axis = drawn.shape.index(max(drawn.shape))
    beside = place[:main_axis] + [(place[main_axis] + 1) % drawn.shape[main_axis]] + place[main_axis + 1:]
    return drawn.at[tuple(place)].set(low).at[tuple(beside)].set(top_value)


def shard_levels(stream_key, extent, pieces, low, high):
    loudness = 1.0
    for position, parts in pieces:
        steps = jax.random.uniform(jax.random.fold_in(jax.random.fold_in(stream_key, 6), position), (parts,), jnp.float32, low / len(pieces), high / len(pieces))
        loudness = loudness * jnp.repeat(jnp.exp(steps), extent[position] // parts).reshape((-1,) + (1,) * (len(extent) - 1 - position))
    return loudness


def scatter_about(own_key, dims, spread, reach, split=(), kind=jnp.bfloat16):
    entries = jax.random.normal(own_key, dims, jnp.float32) * spread
    if len(split) > 0:
        entries = shard_levels(own_key, dims, split, -0.22, 0.18) * entries
    return jnp.clip(entries, min=-reach, max=reach).astype(kind)


def setup_inputs(seed: int = 0) -> dict:
    streams_of = jax.random.split(jax.random.key(seed), 7)
    images = scatter_about(streams_of[0], (IMAGES, IMG * IMG * 3), 1.0, 6.0, ((0, 128),))
    row_list = touch_ends(jax.random.randint(streams_of[1], (IMAGES,), 0, ROWS_DEV), jax.random.fold_in(streams_of[1], 1), 0, ROWS_DEV - 1).astype(jnp.int32)
    labels = touch_ends(jax.random.randint(streams_of[2], (IMAGES,), 0, CLASSES), jax.random.fold_in(streams_of[2], 1), 0, CLASSES - 1).astype(jnp.int32)
    filters = scatter_about(streams_of[3], (6, 6, 3, FILTERS), 108 ** -0.5, 0.625)
    bias = jnp.clip(jax.random.uniform(streams_of[4], (FILTERS,), jnp.float32, -0.8, 0.4), -0.8, 0.4)
    tile_owner = draw_tile_owner(jax.random.fold_in(streams_of[6], 71), 0)
    return dict(images=images, row_list=row_list, labels=labels, filters=filters, bias=bias, tile_owner=tile_owner)


def featurize(block, filters, bias):
    count = block.shape[0]
    pictures = block.reshape(count, IMG, IMG, 3)
    conv = lax.conv_general_dilated(pictures, filters, (2, 2), "VALID", dimension_numbers=("NHWC", "HWIO", "NHWC"), preferred_element_type=jnp.float32)
    active = jnp.maximum(conv + bias, 0.0)
    side = conv.shape[1] // 2
    pooled = jnp.mean(active.reshape(count, 2, side, 2, side, FILTERS), axis=(2, 4))
    return pooled.reshape(count, 4 * FILTERS).astype(jnp.bfloat16)


def reference(images, row_list, labels, filters, bias, tile_owner):
    total = images.shape[0]
    places = jnp.arange(total, dtype=jnp.int32)
    source = (places // ROWS_DEV) * ROWS_DEV + row_list
    chosen = images[source]
    label = labels[source]
    blocks = chosen.reshape(total // 8, 8, chosen.shape[1])
    feats = lax.map(lambda part: featurize(part, filters, bias), blocks).reshape(total, D)
    gram = lax.dot_general(feats, feats, (((0,), (0,)), ((), ())), preferred_element_type=jnp.float32) / total
    targets = jnp.where(label[:, None] == jnp.arange(CLASSES, dtype=jnp.int32)[None, :], 1.0, -1.0).astype(jnp.bfloat16)
    cross = lax.dot_general(feats, targets, (((0,), (0,)), ((), ())), preferred_element_type=jnp.float32) / total
    rows_np, cols_np = np.triu_indices(NB)
    blocked = gram.reshape(NB, TS, NB, TS)
    tiles = blocked[jnp.asarray(rows_np, dtype=jnp.int32), :, jnp.asarray(cols_np, dtype=jnp.int32), :]
    order = jnp.arange(NTILES, dtype=jnp.int32)
    same = tile_owner[:, None] == tile_owner[None, :]
    before = order[:, None] > order[None, :]
    slot = jnp.sum((same & before).astype(jnp.int32), axis=1).astype(jnp.int32)
    gram_tiles = jnp.zeros((N_TILE * MAXT, TS, TS), jnp.float32).at[tile_owner * MAXT + slot].set(tiles)
    return gram_tiles, cross
```

```python
import jax
import jax.numpy as jnp
from jax import lax
from jax.experimental import pallas as pl
from jax.experimental.pallas import tpu as pltpu
from jax.sharding import PartitionSpec as P

ROWS = 96
BLK = 16
NBLK = 6
BF = jnp.bfloat16
F32 = jnp.float32
LAG = 3


def dot(a, b, dims=(((1,), (0,)), ((), ()))):
    return lax.dot_general(a, b, dims, preferred_element_type=F32)


def prep_kernel(rows_ref, labels_ref, img_ref, filt_ref, win_ref, w_ref, sel_ref, lab_ref, nblk_ref, x_ref, pick_ref):
    lanes = lax.broadcasted_iota(jnp.int32, (ROWS, 128), 1)
    subs = lax.broadcasted_iota(jnp.int32, (ROWS, 128), 0)
    hit = rows_ref[...] == lanes
    used = jnp.max(jnp.where(hit, 1.0, 0.0), axis=0, keepdims=True)
    low = lax.broadcasted_iota(jnp.int32, (128, 128), 0)
    high = lax.broadcasted_iota(jnp.int32, (128, 128), 1)
    upto = jnp.where(low <= high, 1.0, 0.0).astype(BF)
    rank = dot(jnp.broadcast_to(used, (16, 128)).astype(BF), upto)[0:1] - 1.0
    rank = rank.astype(jnp.int32)
    compact = jnp.where((subs == rank) & (used > 0.0), 1.0, 0.0).astype(BF)
    sel_ref[:, :ROWS] = dot(jnp.where(hit, 1.0, 0.0).astype(BF), compact, (((1,), (1,)), ((), ()))).astype(BF)
    sel_ref[:, ROWS:] = jnp.zeros((ROWS, 256 - ROWS), BF)
    total = jnp.sum(used).astype(jnp.int32)
    nblk_ref[0, 0] = (total + BLK - 1) // BLK
    label = jnp.sum(jnp.where(hit, labels_ref[...], 0), axis=1, keepdims=True)
    coarse = label // 8
    fine = label - coarse * 8
    lab_ref[...] = jnp.where(lanes == 0, coarse, jnp.where(lanes == 1, fine, 0)).astype(BF)
    take = compact[:, :ROWS]
    rows_i = lax.broadcasted_iota(jnp.int32, (1536, 128), 0)
    cols_i = lax.broadcasted_iota(jnp.int32, (1536, 128), 1)
    d = rows_i // 256
    di = d // 3
    dj = d - 3 * di
    r = rows_i % 256 // 32 - 2 * di
    c = rows_i % 32 - 6 * dj
    ok = (r >= 0) & (r < 6) & (c >= 0) & (c < 18)
    spread = jnp.where(ok & (cols_i == r * 18 + c), 1.0, 0.0).astype(BF)
    for nc in range(4):
        w_ref[nc] = dot(spread, filt_ref[:, nc * 256:(nc + 1) * 256]).astype(BF)
    for part in range(16):
        x_ref[part] = dot(take, img_ref[:, part * 768:(part + 1) * 768]).astype(BF)
    col = lax.broadcasted_iota(jnp.int32, (1, 1280), 1)
    within = col % 32
    source = (col % 128) // 32 * 192 + 18 * (col // 128) + within
    source = jnp.where(within < 30, source, -1)
    place = lax.broadcasted_iota(jnp.int32, (768, 1280), 0)
    pick_ref[...] = jnp.where(place == source, 1.0, 0.0).astype(BF)

    @pl.loop(0, 16)
    def _(part):
        for n in range(5):
            tile = dot(x_ref[part], pick_ref[:, n * 256:(n + 1) * 256]).astype(BF)
            for h in range(2):
                g = 2 * n + h
                for b in range(NBLK):
                    win_ref[part, b, g * 16:(g + 1) * 16, :] = tile[b * 16:(b + 1) * 16, h * 128:(h + 1) * 128]


def prep(images, row_list, labels, flat):
    return pl.pallas_call(
        prep_kernel,
        out_shape=(
            jax.ShapeDtypeStruct((16, NBLK, 160, 128), BF),
            jax.ShapeDtypeStruct((4, 1536, 256), BF),
            jax.ShapeDtypeStruct((ROWS, 256), BF),
            jax.ShapeDtypeStruct((ROWS, 128), BF),
            jax.ShapeDtypeStruct((1, 1), jnp.int32),
        ),
        out_specs=(
            pl.BlockSpec(memory_space=pltpu.VMEM),
            pl.BlockSpec(memory_space=pltpu.VMEM),
            pl.BlockSpec(memory_space=pltpu.VMEM),
            pl.BlockSpec(memory_space=pltpu.VMEM),
            pl.BlockSpec(memory_space=pltpu.SMEM),
        ),
        scratch_shapes=[pltpu.VMEM((16, ROWS, 768), BF), pltpu.VMEM((768, 1280), BF)],
        compiler_params=pltpu.CompilerParams(vmem_limit_bytes=40 * 2**20),
        name="prep",
    )(row_list.reshape(ROWS, 1), jnp.pad(labels, (0, 32)).reshape(1, 128), images, flat)


def conv_kernel(nblk_ref, win_ref, w_ref, sel_ref, bias_ref, out_ref, uniq_ref):
    bias = bias_ref[...]
    floor = jnp.broadcast_to(-bias, (16, 256))
    uniq_ref[...] = jnp.zeros_like(uniq_ref)

    steps = []
    for dd in range(6):
        for w in range(15):
            top = w <= (7 if dd < 3 else 6)
            steps.append((dd, w, 0 if top else 1))

    def block(b, acc):
        total = [[jnp.zeros((16, 256), F32) for _ in range(2)] for _ in range(2)]

        def take(k):
            dd, w, qr = steps[k]
            for m in range(2):
                got = pltpu.matmul_pop(acc[m][k % 8]).reshape(5, 16, 256)
                total[qr][m] = total[qr][m] + jnp.sum(jnp.maximum(got, floor[None]), axis=0)

        for k, (dd, w, qr) in enumerate(steps):
            if w == 0:
                for m in range(2):
                    pltpu.matmul_push_rhs(w_ref[dd * 256:(dd + 1) * 256, :], dd % 2, m)
            for m in range(2):
                lhs = jnp.concatenate(
                    [win_ref[w, b, m * 80:(m + 1) * 80, :], win_ref[w + 1, b, m * 80:(m + 1) * 80, :]], axis=1)
                pltpu.matmul_acc_lhs(acc[m][k % 8], lhs, load_staged_rhs=dd % 2 if w == 0 else None)
            if k >= LAG:
                take(k - LAG)
        for k in range(len(steps) - LAG, len(steps)):
            take(k)
        at = pl.multiple_of(b * 16, 16)
        for qr in range(2):
            for m in range(2):
                q = 2 * qr + m
                mean = (total[qr][m] + 225.0 * bias) * (1.0 / 225.0)
                uniq_ref[pl.ds(at, 16), q * 256:(q + 1) * 256] = mean.astype(BF)

    def scoped(*accs):
        @pl.loop(0, nblk_ref[0, 0])
        def _(b):
            block(b, (accs[:8], accs[8:16]))

        for m in range(2):
            for qr in range(2):
                q = 2 * qr + m
                pltpu.matmul_push_rhs(uniq_ref[:, q * 256:(q + 1) * 256], qr, m)
                pltpu.matmul_acc_lhs(accs[16 + q], sel_ref[...], load_staged_rhs=qr)
        for q in range(4):
            out_ref[:, q * 256:(q + 1) * 256] = pltpu.matmul_pop(accs[16 + q]).astype(BF)

    pl.run_scoped(
        scoped,
        *[pltpu.ACC(m)((80, 256), F32) for m in range(2) for _ in range(8)],
        *[pltpu.ACC(q % 2)((ROWS, 256), F32) for q in range(4)],
    )


def conv(nblk, win, w, sel, bias):
    return pl.pallas_call(
        conv_kernel,
        out_shape=jax.ShapeDtypeStruct((ROWS, 1024), BF),
        in_specs=[pl.BlockSpec(memory_space=pltpu.SMEM)] + [pl.BlockSpec(memory_space=pltpu.VMEM)] * 4,
        out_specs=pl.BlockSpec(memory_space=pltpu.VMEM),
        scratch_shapes=[pltpu.VMEM((256, 1024), BF)],
        compiler_params=pltpu.CompilerParams(vmem_limit_bytes=40 * 2**20),
        cost_estimate=pl.CostEstimate(flops=2 * 86400 * 256 * 256, bytes_accessed=8 * 2**20, transcendentals=0),
        name="conv",
    )(nblk, win, w, sel, bias)


TILES = 16
OWNED = 20
SLOTS = 24
NTILES = 136
GROUP = 1536
CLASSES = 1000
FEAT = 8


def gram_kernel(me_ref, owner_ref, *refs):
    chunks, lab, outs = refs[:4], refs[4], refs[5:5 + FEAT]
    f_ref, ft_ref, target_ref, left_ref, prod_ref, list_i, list_j, sem = refs[5 + FEAT:]
    me_tile = me_ref[0]
    me_feat = me_ref[1]
    copies = []
    for nc in range(4):
        for q in range(4):
            copy = pltpu.make_async_copy(chunks[nc].at[:, q * 256:(q + 1) * 256], f_ref.at[q * 4 + nc], sem.at[q * 4 + nc])
            copy.start()
            copies.append((q * 4 + nc, copy))

    def scan(k, carry):
        i, j, n = carry
        mine = owner_ref[k] == me_tile

        @pl.when(mine)
        def _():
            list_i[n] = i
            list_j[n] = j

        wrap = j == TILES - 1
        i2 = jnp.where(wrap, i + 1, i)
        return i2, jnp.where(wrap, i2, j + 1), n + mine.astype(jnp.int32)

    _, _, owned = lax.fori_loop(0, NTILES, scan, (jnp.int32(0), jnp.int32(0), jnp.int32(0)))

    labels = lab[...].astype(F32)
    label = (labels[:, 0:1] * 8.0 + labels[:, 1:2]).astype(jnp.int32)
    for s in range(4):
        classes = lax.broadcasted_iota(jnp.int32, (GROUP, 256), 1) + 256 * s
        target_ref[:, s * 256:(s + 1) * 256] = jnp.where(label == classes, 1.0, -1.0).astype(BF)
    for t, copy in copies:
        copy.wait()
        ft_ref[t] = f_ref[t].T

    def put(slot, product):
        prod_ref[...] = product
        for k in range(FEAT):
            dz, dy = k // 2, k % 2
            peer = (me_feat // 2 + dz) % 4 * 2 + (me_feat % 2 + dy) % 2
            outs[k][slot] = prod_ref[pl.ds(pl.multiple_of(peer * 32, 32), 32), :]

    @pl.loop(0, owned)
    def _(slot):
        put(slot, dot(ft_ref[list_i[slot]], f_ref[list_j[slot]]))

    @pl.loop(owned, OWNED)
    def _(slot):
        for k in range(FEAT):
            outs[k][slot] = jnp.zeros((32, 256), F32)

    start = pl.multiple_of(me_tile % 8 * 32, 32)
    for f in range(FEAT):
        t = f // 2 * 4 + f % 2 * 2 + me_tile // 8
        left_ref[f * 32:(f + 1) * 32, :] = ft_ref[t, pl.ds(start, 32), :]
    for s in range(4):
        put(OWNED + s, dot(left_ref[...], target_ref[:, s * 256:(s + 1) * 256]))


def gram(me, tile_owner, chunks, lab):
    smem = pl.BlockSpec(memory_space=pltpu.SMEM)
    vmem = pl.BlockSpec(memory_space=pltpu.VMEM)
    return pl.pallas_call(
        gram_kernel,
        out_shape=tuple(jax.ShapeDtypeStruct((SLOTS, 32, 256), F32) for _ in range(FEAT)),
        in_specs=[smem, smem] + [pl.BlockSpec(memory_space=pl.ANY)] * 4 + [vmem],
        out_specs=tuple(vmem for _ in range(FEAT)),
        scratch_shapes=[
            pltpu.VMEM((TILES, GROUP, 256), BF),
            pltpu.VMEM((TILES, 256, GROUP), BF),
            pltpu.VMEM((GROUP, 1024), BF),
            pltpu.VMEM((256, GROUP), BF),
            pltpu.VMEM((256, 256), F32),
            pltpu.SMEM((OWNED,), jnp.int32),
            pltpu.SMEM((OWNED,), jnp.int32),
            pltpu.SemaphoreType.DMA((TILES,)),
        ],
        compiler_params=pltpu.CompilerParams(vmem_limit_bytes=50 * 2**20),
        cost_estimate=pl.CostEstimate(flops=5 * 10**9, bytes_accessed=20 * 2**20, transcendentals=0),
        name="gram",
    )(me, tile_owner, *chunks, lab)


def finish_kernel(*refs):
    parts, gram_ref, cross_ref = refs[:FEAT], refs[FEAT], refs[FEAT + 1]
    scale = 1.0 / 12288.0
    for s in range(SLOTS):
        total = parts[0][s]
        for k in range(1, FEAT):
            total = total + parts[k][s]
        total = total * scale
        if s < OWNED:
            gram_ref[s] = total
        else:
            width = min(256, CLASSES - (s - OWNED) * 256)
            cross_ref[:, (s - OWNED) * 256:(s - OWNED) * 256 + width] = total[:, :width]


def finish(parts):
    return pl.pallas_call(
        finish_kernel,
        out_shape=(jax.ShapeDtypeStruct((OWNED, 32, 256), F32), jax.ShapeDtypeStruct((32, CLASSES), F32)),
        in_specs=[pl.BlockSpec(memory_space=pltpu.VMEM)] * FEAT,
        out_specs=(pl.BlockSpec(memory_space=pltpu.VMEM),) * 2,
        compiler_params=pltpu.CompilerParams(vmem_limit_bytes=40 * 2**20),
        name="finish",
    )(*parts)


def feat_shift(dz, dy):
    return [(z * 2 + y, (z + dz) % 4 * 2 + (y + dy) % 2) for z in range(4) for y in range(2)]


def body(images, row_list, labels, filters, bias, tile_owner):
    flat = jnp.pad(filters.reshape(108, 1024), ((0, 20), (0, 0)))
    win, w, sel, lab, nblk = prep(images, row_list, labels, flat)
    labs = lax.all_gather(lab, "tile", axis=0, tiled=True)
    chunks = []
    for nc in range(4):
        own = conv(nblk, win, w[nc], sel, bias[nc * 256:(nc + 1) * 256].reshape(1, 256))
        chunks.append(lax.all_gather(own, "tile", axis=0, tiled=True))
    me = jnp.stack([lax.axis_index("tile"), lax.axis_index("feat")]).astype(jnp.int32)
    partial = gram(me, tile_owner, chunks, labs)
    parts = [partial[0]]
    for k in range(1, FEAT):
        parts.append(lax.ppermute(partial[k], "feat", feat_shift(k // 2, k % 2)))
    return finish(parts)


def solution(mesh):
    def run(*args):
        return jax.shard_map(
            body,
            mesh=mesh,
            in_specs=(P(("feat", "tile"), None), P(("feat", "tile")), P(("feat", "tile")), P(), P(), P()),
            out_specs=(P("tile", "feat", None), P(("feat", "tile"), None)),
            check_vma=False,
        )(*args)

    return run
```

```python
import jax
import jax.numpy as jnp
from jax import lax
from jax.experimental import pallas as pl
from jax.experimental.pallas import tpu as pltpu
from jax.sharding import PartitionSpec as P

ROWS = 96
BLK = 16
NBLK = 6
BF = jnp.bfloat16
F32 = jnp.float32
LAG = 3


def dot(a, b, dims=(((1,), (0,)), ((), ()))):
    return lax.dot_general(a, b, dims, preferred_element_type=F32)


def prep_kernel(rows_ref, labels_ref, img_ref, filt_ref, win_ref, w_ref, sel_ref, lab_ref, nblk_ref, x_ref, pick_ref):
    lanes = lax.broadcasted_iota(jnp.int32, (ROWS, 128), 1)
    subs = lax.broadcasted_iota(jnp.int32, (ROWS, 128), 0)
    hit = rows_ref[...] == lanes
    used = jnp.max(jnp.where(hit, 1.0, 0.0), axis=0, keepdims=True)
    low = lax.broadcasted_iota(jnp.int32, (128, 128), 0)
    high = lax.broadcasted_iota(jnp.int32, (128, 128), 1)
    upto = jnp.where(low <= high, 1.0, 0.0).astype(BF)
    rank = dot(jnp.broadcast_to(used, (16, 128)).astype(BF), upto)[0:1] - 1.0
    rank = rank.astype(jnp.int32)
    compact = jnp.where((subs == rank) & (used > 0.0), 1.0, 0.0).astype(BF)
    sel_ref[:, :ROWS] = dot(jnp.where(hit, 1.0, 0.0).astype(BF), compact, (((1,), (1,)), ((), ()))).astype(BF)
    sel_ref[:, ROWS:] = jnp.zeros((ROWS, 256 - ROWS), BF)
    total = jnp.sum(used).astype(jnp.int32)
    nblk_ref[0, 0] = (total + BLK - 1) // BLK
    label = jnp.sum(jnp.where(hit, labels_ref[...], 0), axis=1, keepdims=True)
    coarse = label // 8
    fine = label - coarse * 8
    lab_ref[...] = jnp.where(lanes == 0, coarse, jnp.where(lanes == 1, fine, 0)).astype(BF)
    take = compact[:, :ROWS]
    rows_i = lax.broadcasted_iota(jnp.int32, (1536, 128), 0)
    cols_i = lax.broadcasted_iota(jnp.int32, (1536, 128), 1)
    d = rows_i // 256
    di = d // 3
    dj = d - 3 * di
    r = rows_i % 256 // 32 - 2 * di
    c = rows_i % 32 - 6 * dj
    ok = (r >= 0) & (r < 6) & (c >= 0) & (c < 18)
    spread = jnp.where(ok & (cols_i == r * 18 + c), 1.0, 0.0).astype(BF)
    for nc in range(4):
        w_ref[nc] = dot(spread, filt_ref[:, nc * 256:(nc + 1) * 256]).astype(BF)
    for part in range(16):
        x_ref[part] = dot(take, img_ref[:, part * 768:(part + 1) * 768]).astype(BF)
    col = lax.broadcasted_iota(jnp.int32, (1, 1280), 1)
    within = col % 32
    source = (col % 128) // 32 * 192 + 18 * (col // 128) + within
    source = jnp.where(within < 30, source, -1)
    place = lax.broadcasted_iota(jnp.int32, (768, 1280), 0)
    pick_ref[...] = jnp.where(place == source, 1.0, 0.0).astype(BF)

    @pl.loop(0, 16)
    def _(part):
        for n in range(5):
            tile = dot(x_ref[part], pick_ref[:, n * 256:(n + 1) * 256]).astype(BF)
            for h in range(2):
                g = 2 * n + h
                for b in range(NBLK):
                    win_ref[part, b, g * 16:(g + 1) * 16, :] = tile[b * 16:(b + 1) * 16, h * 128:(h + 1) * 128]


def prep(images, row_list, labels, flat):
    return pl.pallas_call(
        prep_kernel,
        out_shape=(
            jax.ShapeDtypeStruct((16, NBLK, 160, 128), BF),
            jax.ShapeDtypeStruct((4, 1536, 256), BF),
            jax.ShapeDtypeStruct((ROWS, 256), BF),
            jax.ShapeDtypeStruct((ROWS, 128), BF),
            jax.ShapeDtypeStruct((1, 1), jnp.int32),
        ),
        out_specs=(
            pl.BlockSpec(memory_space=pltpu.VMEM),
            pl.BlockSpec(memory_space=pltpu.VMEM),
            pl.BlockSpec(memory_space=pltpu.VMEM),
            pl.BlockSpec(memory_space=pltpu.VMEM),
            pl.BlockSpec(memory_space=pltpu.SMEM),
        ),
        scratch_shapes=[pltpu.VMEM((16, ROWS, 768), BF), pltpu.VMEM((768, 1280), BF)],
        compiler_params=pltpu.CompilerParams(vmem_limit_bytes=40 * 2**20),
        name="prep",
    )(row_list.reshape(ROWS, 1), jnp.pad(labels, (0, 32)).reshape(1, 128), images, flat)


def conv_kernel(nblk_ref, win_ref, w_ref, sel_ref, bias_ref, lab_ref, *refs):
    out_ref, uniq_ref = refs[-2:]
    count = w_ref.shape[0]
    uniq_ref[...] = jnp.zeros_like(uniq_ref)
    if out_ref.shape[1] > count * 1024:
        out_ref[:, count * 1024:] = lab_ref[...]
    steps = []
    for d in range(6):
        for w in range(15):
            steps.append((d, w, 0 if w <= (7 if d < 3 else 6) else 1))

    def block(nc, b, bias, floor, acc):
        total = [[jnp.zeros((16, 256), F32) for _ in range(2)] for _ in range(2)]

        def take(k):
            qr = steps[k][2]
            for m in range(2):
                got = pltpu.matmul_pop(acc[m][k % 8]).reshape(5, 16, 256)
                total[qr][m] = total[qr][m] + jnp.sum(jnp.maximum(got, floor[None]), axis=0)

        for k, (d, w, _) in enumerate(steps):
            if w == 0:
                for m in range(2):
                    pltpu.matmul_push_rhs(w_ref[nc, d * 256:(d + 1) * 256, :], d % 2, m)
            for m in range(2):
                rows = slice(m * 80, (m + 1) * 80)
                lhs = jnp.concatenate([win_ref[w, b, rows, :], win_ref[w + 1, b, rows, :]], axis=1)
                pltpu.matmul_acc_lhs(acc[m][k % 8], lhs, load_staged_rhs=d % 2 if w == 0 else None)
            if k >= LAG:
                take(k - LAG)
        for k in range(len(steps) - LAG, len(steps)):
            take(k)
        at = pl.multiple_of(b * 16, 16)
        for qr in range(2):
            for m in range(2):
                q = 2 * qr + m
                mean = (total[qr][m] + 225.0 * bias) * (1.0 / 225.0)
                uniq_ref[pl.ds(at, 16), q * 256:(q + 1) * 256] = mean.astype(BF)

    def scoped(*accs):
        @pl.loop(0, count)
        def _(nc):
            bias = bias_ref[nc]
            floor = jnp.broadcast_to(-bias, (16, 256))

            @pl.loop(0, nblk_ref[0, 0])
            def _(b):
                block(nc, b, bias, floor, (accs[:8], accs[8:16]))

            for m in range(2):
                for qr in range(2):
                    q = 2 * qr + m
                    pltpu.matmul_push_rhs(uniq_ref[:, q * 256:(q + 1) * 256], qr, m)
                    pltpu.matmul_acc_lhs(accs[16 + q], sel_ref[...], load_staged_rhs=qr)
            for q in range(4):
                at = pl.multiple_of(nc * 1024 + q * 256, 256)
                out_ref[:, pl.ds(at, 256)] = pltpu.matmul_pop(accs[16 + q]).astype(BF)

    pl.run_scoped(
        scoped,
        *[pltpu.ACC(m)((80, 256), F32) for m in range(2) for _ in range(8)],
        *[pltpu.ACC(q % 2)((ROWS, 256), F32) for q in range(4)],
    )


def conv(nblk, win, w, sel, bias, lab, extra, after=()):
    count = w.shape[0]
    return pl.pallas_call(
        conv_kernel,
        out_shape=jax.ShapeDtypeStruct((ROWS, count * 1024 + extra), BF),
        in_specs=[pl.BlockSpec(memory_space=pltpu.SMEM)] + [pl.BlockSpec(memory_space=pltpu.VMEM)] * 5
        + [pl.BlockSpec(memory_space=pl.ANY)] * len(after),
        out_specs=pl.BlockSpec(memory_space=pltpu.VMEM),
        scratch_shapes=[pltpu.VMEM((256, 1024), BF)],
        compiler_params=pltpu.CompilerParams(vmem_limit_bytes=40 * 2**20),
        cost_estimate=pl.CostEstimate(flops=count * 2 * 86400 * 256 * 256, bytes_accessed=8 * 2**20, transcendentals=0),
        name="conv",
    )(nblk, win, w, sel, bias, lab, *after)


TILES = 16
OWNED = 20
SLOTS = 24
NTILES = 136
GROUP = 1536
CLASSES = 1000
FEAT = 8


BLOCKS = ((0, 96), (96, 96), (192, 96), (288, 96), (384, 96), (480, 96), (576, 96), (672, 96), (768, 384), (1152, 288), (1440, 96))


def gram_kernel(me_ref, owner_ref, *refs):
    n = len(BLOCKS)
    parts, (out_ref, peak_ref) = (refs[:n], refs[n:2 * n]), refs[2 * n:2 * n + 2]
    f_ref, ft_ref, lab, target_ref, left_ref, list_i, list_j, sem = refs[2 * n + 2:]
    me_tile = me_ref[0]
    peak_ref[...] = jnp.zeros_like(peak_ref)
    copies = {}
    for part in range(2):
        for local in range(2):
            for q in range(4):
                tile = q * 4 + part * 2 + local
                cols = slice(local * 1024 + q * 256, local * 1024 + (q + 1) * 256)
                copies[tile] = [
                    pltpu.make_async_copy(ref.at[:, cols], f_ref.at[tile, start:start + size], sem.at[tile])
                    for ref, (start, size) in zip(parts[part], BLOCKS)
                ]
    copies[TILES] = [
        pltpu.make_async_copy(ref.at[:, 2048:], lab.at[start:start + size], sem.at[TILES])
        for ref, (start, size) in zip(parts[0], BLOCKS)
    ]
    for group in copies.values():
        for copy in group:
            copy.start()

    def scan(k, carry):
        i, j, n = carry
        mine = owner_ref[k] == me_tile

        @pl.when(mine)
        def _():
            list_i[n] = i
            list_j[n] = j

        wrap = j == TILES - 1
        i2 = jnp.where(wrap, i + 1, i)
        return i2, jnp.where(wrap, i2, j + 1), n + mine.astype(jnp.int32)

    _, _, owned = lax.fori_loop(0, NTILES, scan, (jnp.int32(0), jnp.int32(0), jnp.int32(0)))

    for copy in copies[TILES]:
        copy.wait()
    labels = lab[...].astype(F32)
    label = (labels[:, 0:1] * 8.0 + labels[:, 1:2]).astype(jnp.int32)
    for s in range(4):
        classes = lax.broadcasted_iota(jnp.int32, (GROUP, 256), 1) + 256 * s
        target_ref[:, s * 256:(s + 1) * 256] = jnp.where(label == classes, 1.0, -1.0).astype(BF)
    for t in range(TILES):
        for copy in copies[t]:
            copy.wait()
        ft_ref[t] = f_ref[t].T

    def put(slot, product):
        peak_ref[...] = jnp.maximum(peak_ref[...], jnp.max(jnp.abs(product).reshape(32, 8, 256), axis=0))
        for k in range(FEAT):
            out_ref[k, slot] = product[k * 32:(k + 1) * 32, :]

    @pl.loop(0, owned)
    def _(slot):
        put(slot, dot(ft_ref[list_i[slot]], f_ref[list_j[slot]]))

    @pl.loop(owned, OWNED)
    def _(slot):
        for k in range(FEAT):
            out_ref[k, slot] = jnp.zeros((32, 256), F32)

    start = pl.multiple_of(me_tile % 8 * 32, 32)
    for f in range(FEAT):
        t = f // 2 * 4 + f % 2 * 2 + me_tile // 8
        left_ref[f * 32:(f + 1) * 32, :] = ft_ref[t, pl.ds(start, 32), :]
    for s in range(4):
        put(OWNED + s, dot(left_ref[...], target_ref[:, s * 256:(s + 1) * 256]))


def gram(me, tile_owner, parts):
    smem = pl.BlockSpec(memory_space=pltpu.SMEM)
    vmem = pl.BlockSpec(memory_space=pltpu.VMEM)
    return pl.pallas_call(
        gram_kernel,
        out_shape=(jax.ShapeDtypeStruct((FEAT, SLOTS, 32, 256), F32), jax.ShapeDtypeStruct((8, 256), F32)),
        in_specs=[smem, smem] + [pl.BlockSpec(memory_space=pl.ANY)] * (2 * len(BLOCKS)),
        out_specs=(vmem, vmem),
        scratch_shapes=[
            pltpu.VMEM((TILES, GROUP, 256), BF),
            pltpu.VMEM((TILES, 256, GROUP), BF),
            pltpu.VMEM((GROUP, 128), BF),
            pltpu.VMEM((GROUP, 1024), BF),
            pltpu.VMEM((256, GROUP), BF),
            pltpu.SMEM((OWNED,), jnp.int32),
            pltpu.SMEM((OWNED,), jnp.int32),
            pltpu.SemaphoreType.DMA((TILES + 1,)),
        ],
        compiler_params=pltpu.CompilerParams(vmem_limit_bytes=50 * 2**20),
        cost_estimate=pl.CostEstimate(flops=5 * 10**9, bytes_accessed=20 * 2**20, transcendentals=0),
        name="gram",
    )(me, tile_owner, *parts[0], *parts[1])


HALF = jnp.float16


def exchange(partial, peak):
    exponent = jnp.floor(jnp.log2(jnp.maximum(jnp.max(peak), 1e-30)))
    coded = (partial * jnp.exp2(13.0 - exponent)).astype(HALF)
    note = jnp.broadcast_to(exponent.astype(HALF), (FEAT, 1, 32, 256))
    got = lax.all_to_all(jnp.concatenate([coded, note], axis=1), "feat", split_axis=0, concat_axis=0, tiled=True)
    back = jnp.exp2(got[:, SLOTS:, :1, :1].astype(F32) - 13.0) * (1.0 / 12288.0)
    total = jnp.sum(got[:, :SLOTS].astype(F32) * back, axis=0)
    return total


def finish(total):
    cross = total[OWNED:].transpose(1, 0, 2).reshape(32, 1024)[:, :CLASSES]
    return total[:OWNED], cross


def hop(dy=0, dx=0, core=0):
    def index(y, x, c):
        return (y % 2 * 4 + x % 4) * 2 + c % 2

    return [(index(y, x, c), index(y + dy, x + dx, c + core)) for y in range(2) for x in range(4) for c in range(2)]


def onward():
    return [(s, d) if s % 2 == 0 else (s, e) for (s, d), (_, e) in zip(hop(dx=1), hop(dx=-1))]


def send(block, perm):
    return lax.ppermute(block, "tile", perm)


def spread_first(own):
    left = send(own, hop(dx=1))
    right = send(own, hop(dx=-1))
    over = send(own, hop(dy=1))
    return own, over, left, right


def spread_second(first):
    own, over, left, right = first
    even = lax.axis_index("tile") % 2 == 0
    far = send(jnp.where(even, left, right), onward())
    over_left = send(over, hop(dx=1))
    over_right = send(over, hop(dx=-1))
    swap_a = send(jnp.concatenate([own, over, left, right], axis=0), hop(core=1))
    return far, over_left, over_right, swap_a


def spread_third(first, second):
    own, over, left, right = first
    far, over_left, over_right, swap_a = second
    even = lax.axis_index("tile") % 2 == 0
    over_far = send(jnp.where(even, over_left, over_right), onward())
    swap_b = send(jnp.concatenate([over_left, over_right, far], axis=0), hop(core=1))
    swap_c = send(over_far, hop(core=1))
    return [own, over, left, right, over_left, over_right, far, over_far, swap_a, swap_b, swap_c]


def body(images, row_list, labels, filters, bias, tile_owner):
    flat = jnp.pad(filters.reshape(108, 1024), ((0, 20), (0, 0)))
    win, w, sel, lab, nblk = prep(images, row_list, labels, flat)
    bias4 = bias.reshape(4, 1, 256)
    own_a = conv(nblk, win, w[0:2], sel, bias4[0:2], lab, 128)
    first_a = spread_first(own_a)
    own_b2 = conv(nblk, win, w[2:3], sel, bias4[2:3], lab, 0, (own_a,))
    second_a = spread_second(first_a)
    own_b3 = conv(nblk, win, w[3:4], sel, bias4[3:4], lab, 0, first_a[1:])
    own_b = jnp.concatenate([own_b2, own_b3], axis=1)
    own_b, far, over_left, over_right = lax.optimization_barrier((own_b,) + second_a[:3])
    second_a = (far, over_left, over_right, second_a[3])
    first_b = spread_first(own_b)
    part_a = spread_third(first_a, second_a)
    second_b = spread_second(first_b)
    part_b = spread_third(first_b, second_b)
    me = jnp.stack([lax.axis_index("tile"), lax.axis_index("feat")]).astype(jnp.int32)
    partial, peak = gram(me, tile_owner, (part_a, part_b))
    return finish(exchange(partial, peak))


def solution(mesh):
    def run(*args):
        return jax.shard_map(
            body,
            mesh=mesh,
            in_specs=(P(("feat", "tile"), None), P(("feat", "tile")), P(("feat", "tile")), P(), P(), P()),
            out_specs=(P("tile", "feat", None), P(("feat", "tile"), None)),
            check_vma=False,
        )(*args)

    return run
```

```python
import functools

import jax
import jax.numpy as jnp
from jax import lax
from jax.experimental import pallas as pl
from jax.experimental.pallas import tpu as pltpu
from jax.sharding import PartitionSpec as P

ROWS = 96
BLK = 16
NBLK = 6
BF = jnp.bfloat16
F32 = jnp.float32
LAG = 3


def dot(a, b, dims=(((1,), (0,)), ((), ()))):
    return lax.dot_general(a, b, dims, preferred_element_type=F32)


def prep_kernel(rows_ref, labels_ref, filt_ref, img_hbm, win_ref, w_ref, sel_ref, lab_ref, nblk_ref, img_ref, x_ref, pick_ref, flat_ref, sem):
    fetch = pltpu.make_async_copy(img_hbm, img_ref, sem)
    fetch.start()
    flat_ref[...] = jnp.zeros_like(flat_ref)
    for i in range(6):
        for j in range(6):
            p = 6 * i + j
            flat_ref[3 * p:3 * p + 3, :] = filt_ref[i, j].astype(F32)
    rows_i = lax.broadcasted_iota(jnp.int32, (1536, 128), 0)
    cols_i = lax.broadcasted_iota(jnp.int32, (1536, 128), 1)
    d = rows_i // 256
    di = d // 3
    dj = d - 3 * di
    r = rows_i % 256 // 32 - 2 * di
    c = rows_i % 32 - 6 * dj
    ok = (r >= 0) & (r < 6) & (c >= 0) & (c < 18)
    spread = jnp.where(ok & (cols_i == r * 18 + c), 1.0, 0.0).astype(BF)
    for nc in range(4):
        w_ref[nc] = dot(spread, flat_ref[:, nc * 256:(nc + 1) * 256].astype(BF)).astype(BF)

    lanes = lax.broadcasted_iota(jnp.int32, (ROWS, 128), 1)
    subs = lax.broadcasted_iota(jnp.int32, (ROWS, 128), 0)
    rows = jnp.broadcast_to(rows_ref[...], (128, 128)).astype(F32).T[:ROWS]
    hit = rows.astype(jnp.int32) == lanes
    used = jnp.max(jnp.where(hit, 1.0, 0.0), axis=0, keepdims=True)
    low = lax.broadcasted_iota(jnp.int32, (128, 128), 0)
    high = lax.broadcasted_iota(jnp.int32, (128, 128), 1)
    upto = jnp.where(low <= high, 1.0, 0.0).astype(BF)
    rank = dot(jnp.broadcast_to(used, (16, 128)).astype(BF), upto)[0:1] - 1.0
    rank = rank.astype(jnp.int32)
    compact = jnp.where((subs == rank) & (used > 0.0), 1.0, 0.0).astype(BF)
    sel_ref[:, :ROWS] = dot(jnp.where(hit, 1.0, 0.0).astype(BF), compact, (((1,), (1,)), ((), ()))).astype(BF)
    sel_ref[:, ROWS:] = jnp.zeros((ROWS, 256 - ROWS), BF)
    total = jnp.sum(used).astype(jnp.int32)
    nblk_ref[0, 0] = (total + BLK - 1) // BLK
    label = jnp.sum(jnp.where(hit, labels_ref[...], 0), axis=1, keepdims=True)
    coarse = label // 8
    fine = label - coarse * 8
    lab_ref[...] = jnp.where(lanes == 0, coarse, jnp.where(lanes == 1, fine, 0)).astype(BF)
    take = compact[:, :ROWS]
    col = lax.broadcasted_iota(jnp.int32, (1, 1280), 1)
    within = col % 32
    source = (col % 128) // 32 * 192 + 18 * (col // 128) + within
    source = jnp.where(within < 30, source, -1)
    place = lax.broadcasted_iota(jnp.int32, (768, 1280), 0)
    pick_ref[...] = jnp.where(place == source, 1.0, 0.0).astype(BF)
    fetch.wait()
    for part in range(16):
        x_ref[part * ROWS:(part + 1) * ROWS, :] = dot(take, img_ref[:, part * 768:(part + 1) * 768]).astype(BF)

    @pl.loop(0, 5)
    def _(n):
        tile = dot(x_ref[...], pick_ref[:, pl.ds(pl.multiple_of(n * 256, 256), 256)]).astype(BF)
        for h in range(2):
            at = pl.multiple_of((2 * n + h) * 16, 16)
            for part in range(16):
                for b in range(NBLK):
                    row = part * ROWS + b * 16
                    win_ref[part, b, pl.ds(at, 16), :] = tile[row:row + 16, h * 128:(h + 1) * 128]


def prep(images, row_list, labels, filters):
    vmem = pl.BlockSpec(memory_space=pltpu.VMEM)
    return pl.pallas_call(
        prep_kernel,
        out_shape=(
            jax.ShapeDtypeStruct((16, NBLK, 160, 128), BF),
            jax.ShapeDtypeStruct((4, 1536, 256), BF),
            jax.ShapeDtypeStruct((ROWS, 256), BF),
            jax.ShapeDtypeStruct((ROWS, 128), BF),
            jax.ShapeDtypeStruct((1, 1), jnp.int32),
        ),
        in_specs=[vmem, vmem, vmem, pl.BlockSpec(memory_space=pl.ANY)],
        out_specs=(vmem, vmem, vmem, vmem, pl.BlockSpec(memory_space=pltpu.SMEM)),
        scratch_shapes=[
            pltpu.VMEM((ROWS, 12288), BF),
            pltpu.VMEM((16 * ROWS, 768), BF),
            pltpu.VMEM((768, 1280), BF),
            pltpu.VMEM((128, 1024), F32),
            pltpu.SemaphoreType.DMA,
        ],
        compiler_params=pltpu.CompilerParams(vmem_limit_bytes=40 * 2**20),
        name="prep",
    )(jnp.pad(row_list, (0, 32)).reshape(1, 128), jnp.pad(labels, (0, 32)).reshape(1, 128), filters, images)


def conv_kernel(first, count, nblk_ref, win_ref, w_ref, sel_ref, bias_ref, lab_ref, *refs):
    out_ref, uniq_ref = refs[-2:]
    uniq_ref[...] = jnp.zeros_like(uniq_ref)
    if out_ref.shape[1] > count * 1024:
        out_ref[:, count * 1024:] = lab_ref[...]
    steps = []
    for d in range(6):
        for w in range(15):
            steps.append((d, w, 0 if w <= (7 if d < 3 else 6) else 1))

    def block(nc, b, bias, floor, acc):
        total = [[jnp.zeros((16, 256), F32) for _ in range(2)] for _ in range(2)]

        def take(k):
            qr = steps[k][2]
            for m in range(2):
                got = pltpu.matmul_pop(acc[m][k % 8]).reshape(5, 16, 256)
                total[qr][m] = total[qr][m] + jnp.sum(jnp.maximum(got, floor[None]), axis=0)

        for k, (d, w, _) in enumerate(steps):
            if w == 0:
                for m in range(2):
                    pltpu.matmul_push_rhs(w_ref[first + nc, d * 256:(d + 1) * 256, :], d % 2, m)
            for m in range(2):
                rows = slice(m * 80, (m + 1) * 80)
                lhs = jnp.concatenate([win_ref[w, b, rows, :], win_ref[w + 1, b, rows, :]], axis=1)
                pltpu.matmul_acc_lhs(acc[m][k % 8], lhs, load_staged_rhs=d % 2 if w == 0 else None)
            if k >= LAG:
                take(k - LAG)
        for k in range(len(steps) - LAG, len(steps)):
            take(k)
        at = pl.multiple_of(b * 16, 16)
        for qr in range(2):
            for m in range(2):
                q = 2 * qr + m
                mean = (total[qr][m] + 225.0 * bias) * (1.0 / 225.0)
                uniq_ref[pl.ds(at, 16), q * 256:(q + 1) * 256] = mean.astype(BF)

    def scoped(*accs):
        @pl.loop(0, count)
        def _(nc):
            bias = bias_ref[first + nc]
            floor = jnp.broadcast_to(-bias, (16, 256))

            @pl.loop(0, nblk_ref[0, 0])
            def _(b):
                block(nc, b, bias, floor, (accs[:8], accs[8:16]))

            for m in range(2):
                for qr in range(2):
                    q = 2 * qr + m
                    pltpu.matmul_push_rhs(uniq_ref[:, q * 256:(q + 1) * 256], qr, m)
                    pltpu.matmul_acc_lhs(accs[16 + q], sel_ref[...], load_staged_rhs=qr)
            for q in range(4):
                at = pl.multiple_of(nc * 1024 + q * 256, 256)
                out_ref[:, pl.ds(at, 256)] = pltpu.matmul_pop(accs[16 + q]).astype(BF)

    pl.run_scoped(
        scoped,
        *[pltpu.ACC(m)((80, 256), F32) for m in range(2) for _ in range(8)],
        *[pltpu.ACC(q % 2)((ROWS, 256), F32) for q in range(4)],
    )


def conv(first, count, nblk, win, w, sel, bias, lab, extra, after=()):
    return pl.pallas_call(
        functools.partial(conv_kernel, first, count),
        out_shape=jax.ShapeDtypeStruct((ROWS, count * 1024 + extra), BF),
        in_specs=[pl.BlockSpec(memory_space=pltpu.SMEM)] + [pl.BlockSpec(memory_space=pltpu.VMEM)] * 5
        + [pl.BlockSpec(memory_space=pl.ANY)] * len(after),
        out_specs=pl.BlockSpec(memory_space=pltpu.VMEM),
        scratch_shapes=[pltpu.VMEM((256, 1024), BF)],
        compiler_params=pltpu.CompilerParams(vmem_limit_bytes=40 * 2**20),
        cost_estimate=pl.CostEstimate(flops=count * 2 * 86400 * 256 * 256, bytes_accessed=8 * 2**20, transcendentals=0),
        name="conv",
    )(nblk, win, w, sel, bias, lab, *after)


TILES = 16
OWNED = 20
SLOTS = 25
NOTE = 4
FIRST = 5
NTILES = 136
GROUP = 1536
CLASSES = 1000
FEAT = 8


BLOCKS = ((0, 96), (96, 96), (192, 96), (288, 96), (384, 96), (480, 96), (576, 96), (672, 96), (768, 384), (1152, 288), (1440, 96))


def gram_kernel(me_ref, owner_ref, *refs):
    n = len(BLOCKS)
    parts, (out_ref, peak_ref) = (refs[:n], refs[n:2 * n]), refs[2 * n:2 * n + 2]
    fa_ref, fb_ref, ft_ref, target_ref, left_ref, list_i, list_j, sem = refs[2 * n + 2:]
    held = (fa_ref, fb_ref)
    me_tile = me_ref[0]
    copies = [
        [
            pltpu.make_async_copy(ref, held[part].at[start:start + size], sem.at[part * n + k])
            for k, (ref, (start, size)) in enumerate(zip(parts[part], BLOCKS))
        ]
        for part in range(2)
    ]
    for group in copies:
        for copy in group:
            copy.start()

    def scan(k, carry):
        i, j, n = carry
        mine = owner_ref[k] == me_tile

        @pl.when(mine)
        def _():
            list_i[n] = i
            list_j[n] = j

        wrap = j == TILES - 1
        i2 = jnp.where(wrap, i + 1, i)
        return i2, jnp.where(wrap, i2, j + 1), n + mine.astype(jnp.int32)

    _, _, owned = lax.fori_loop(0, NTILES, scan, (jnp.int32(0), jnp.int32(0), jnp.int32(0)))
    peak_ref[...] = jnp.zeros_like(peak_ref)

    @pl.loop(owned, OWNED)
    def _(slot):
        for k in range(FEAT):
            out_ref[k, slot + FIRST] = jnp.zeros((32, 256), F32)

    for part in range(2):
        for copy in copies[part]:
            copy.wait()
        for local in range(2):
            for q in range(4):
                cols = slice(local * 1024 + q * 256, local * 1024 + (q + 1) * 256)
                ft_ref[q * 4 + part * 2 + local] = held[part][:, cols].T
    digit = lax.broadcasted_iota(jnp.int32, (128, 256), 0)
    weight = jnp.where(digit == 0, 8.0, jnp.where(digit == 1, 1.0, 0.0)).astype(BF)
    label = dot(fa_ref[:, 2048:], weight)
    classes = lax.broadcasted_iota(jnp.int32, (GROUP, 256), 1).astype(F32)
    for s in range(4):
        target_ref[:, s * 256:(s + 1) * 256] = jnp.where(label == classes + 256.0 * s, 1.0, -1.0).astype(BF)

    def put(slot, product):
        peak_ref[...] = jnp.maximum(peak_ref[...], jnp.max(jnp.abs(product).reshape(32, 8, 256), axis=0))
        for k in range(FEAT):
            out_ref[k, slot] = product[k * 32:(k + 1) * 32, :]

    start = pl.multiple_of(me_tile % 8 * 32, 32)
    for f in range(FEAT):
        t = f // 2 * 4 + f % 2 * 2 + me_tile // 8
        left_ref[f * 32:(f + 1) * 32, :] = ft_ref[t, pl.ds(start, 32), :]
    for s in range(4):
        put(s, dot(left_ref[...], target_ref[:, s * 256:(s + 1) * 256]))
    for s in range(0, FEAT, 2):
        out_ref[s:s + 2, NOTE] = jnp.zeros((2, 32, 256), F32)

    @pl.loop(0, owned)
    def _(slot):
        j = list_j[slot]
        at = pl.multiple_of(j % 2 * 1024 + j // 4 * 256, 256)
        second = j % 4 >= 2

        @pl.when(second)
        def _():
            put(slot + FIRST, dot(ft_ref[list_i[slot]], fb_ref[:, pl.ds(at, 256)]))

        @pl.when(jnp.logical_not(second))
        def _():
            put(slot + FIRST, dot(ft_ref[list_i[slot]], fa_ref[:, pl.ds(at, 256)]))


def gram(me, tile_owner, parts):
    smem = pl.BlockSpec(memory_space=pltpu.SMEM)
    vmem = pl.BlockSpec(memory_space=pltpu.VMEM)
    return pl.pallas_call(
        gram_kernel,
        out_shape=(jax.ShapeDtypeStruct((FEAT, SLOTS, 32, 256), F32), jax.ShapeDtypeStruct((8, 256), F32)),
        in_specs=[smem, smem] + [pl.BlockSpec(memory_space=pltpu.HBM)] * (2 * len(BLOCKS)),
        out_specs=(vmem, vmem),
        scratch_shapes=[
            pltpu.VMEM((GROUP, 2176), BF),
            pltpu.VMEM((GROUP, 2048), BF),
            pltpu.VMEM((TILES, 256, GROUP), BF),
            pltpu.VMEM((GROUP, 1024), BF),
            pltpu.VMEM((256, GROUP), BF),
            pltpu.SMEM((OWNED,), jnp.int32),
            pltpu.SMEM((OWNED,), jnp.int32),
            pltpu.SemaphoreType.DMA((2 * len(BLOCKS),)),
        ],
        compiler_params=pltpu.CompilerParams(vmem_limit_bytes=56 * 2**20),
        cost_estimate=pl.CostEstimate(flops=5 * 10**9, bytes_accessed=20 * 2**20, transcendentals=0),
        name="gram",
    )(me, tile_owner, *parts[0], *parts[1])


HALF = jnp.float16


STEPS = (8, 12, 20)


def exchange(partial, peak, owned):
    exponent = jnp.floor(jnp.log2(jnp.maximum(jnp.max(peak), 1e-30)))
    scale = jnp.exp2(13.0 - exponent)

    def some(count, partial):
        used = partial[:, :FIRST + count]
        note = lax.broadcasted_iota(jnp.int32, used.shape, 1) == NOTE
        coded = jnp.where(note, exponent, used * scale).astype(HALF)
        got = lax.all_to_all(coded, "feat", split_axis=0, concat_axis=0, tiled=True)
        back = jnp.exp2(got[:, NOTE:FIRST, :1, :1].astype(F32) - 13.0) * (1.0 / 12288.0)
        total = jnp.sum(got.astype(F32) * back, axis=0)
        cross = total[:NOTE].transpose(1, 0, 2).reshape(32, 1024)[:, :CLASSES]
        return jnp.pad(total[FIRST:], ((0, OWNED - count), (0, 0), (0, 0))), cross

    level = sum((owned > step).astype(jnp.int32) for step in STEPS[:-1])
    return lax.switch(level, [functools.partial(some, step) for step in STEPS], partial)


def hop(dy=0, dx=0, core=0):
    def index(y, x, c):
        return (y % 2 * 4 + x % 4) * 2 + c % 2

    return [(index(y, x, c), index(y + dy, x + dx, c + core)) for y in range(2) for x in range(4) for c in range(2)]


def onward():
    return [(s, d) if s % 2 == 0 else (s, e) for (s, d), (_, e) in zip(hop(dx=1), hop(dx=-1))]


def send(block, perm):
    return lax.ppermute(block, "tile", perm)


def spread_first(own):
    left = send(own, hop(dx=1))
    right = send(own, hop(dx=-1))
    over = send(own, hop(dy=1))
    return own, over, left, right


def spread_second(first):
    own, over, left, right = first
    even = lax.axis_index("tile") % 2 == 0
    far = send(jnp.where(even, left, right), onward())
    over_left = send(over, hop(dx=1))
    over_right = send(over, hop(dx=-1))
    swap_a = send(jnp.concatenate([own, over, left, right], axis=0), hop(core=1))
    return far, over_left, over_right, swap_a


def spread_third(first, second):
    own, over, left, right = first
    far, over_left, over_right, swap_a = second
    even = lax.axis_index("tile") % 2 == 0
    over_far = send(jnp.where(even, over_left, over_right), onward())
    swap_b = send(jnp.concatenate([over_left, over_right, far], axis=0), hop(core=1))
    swap_c = send(over_far, hop(core=1))
    return [own, over, left, right, over_left, over_right, far, over_far, swap_a, swap_b, swap_c]


def body(images, row_list, labels, filters, bias, tile_owner):
    win, w, sel, lab, nblk = prep(images, row_list, labels, filters)
    bias4 = bias.reshape(4, 1, 256)
    own_a = conv(0, 2, nblk, win, w, sel, bias4, lab, 128)
    first_a = spread_first(own_a)
    own_b2 = conv(2, 1, nblk, win, w, sel, bias4, lab, 0, (own_a,))
    second_a = spread_second(first_a)
    own_b3 = conv(3, 1, nblk, win, w, sel, bias4, lab, 0, first_a[1:])
    own_b = jnp.concatenate([own_b2, own_b3], axis=1)
    own_b, far, over_left, over_right = lax.optimization_barrier((own_b,) + second_a[:3])
    second_a = (far, over_left, over_right, second_a[3])
    first_b = spread_first(own_b)
    part_a = spread_third(first_a, second_a)
    second_b = spread_second(first_b)
    part_b = spread_third(first_b, second_b)
    me = jnp.stack([lax.axis_index("tile"), lax.axis_index("feat")]).astype(jnp.int32)
    partial, peak = gram(me, tile_owner, (part_a, part_b))
    owned = jnp.sum((tile_owner == me[0]).astype(jnp.int32))
    return exchange(partial, peak, owned)


def solution(mesh):
    def run(*args):
        return jax.shard_map(
            body,
            mesh=mesh,
            in_specs=(P(("feat", "tile"), None), P(("feat", "tile")), P(("feat", "tile")), P(), P(), P()),
            out_specs=(P("tile", "feat", None), P(("feat", "tile"), None)),
            check_vma=False,
        )(*args)

    return run
```

```python
import functools

import jax
import jax.numpy as jnp
from jax import lax
from jax.experimental import pallas as pl
from jax.experimental.pallas import tpu as pltpu
from jax.sharding import PartitionSpec as P

ROWS = 96
BLK = 16
NBLK = 6
BF = jnp.bfloat16
F32 = jnp.float32
LAG = 3


def dot(a, b, dims=(((1,), (0,)), ((), ()))):
    return lax.dot_general(a, b, dims, preferred_element_type=F32)


def prep_kernel(rows_ref, labels_ref, filt_ref, img_hbm, win_ref, w_ref, sel_ref, lab_ref, nblk_ref, img_ref, x_ref, pick_ref, flat_ref, sem):
    fetch = pltpu.make_async_copy(img_hbm, img_ref, sem)
    fetch.start()
    flat_ref[...] = jnp.zeros_like(flat_ref)
    for i in range(6):
        for j in range(6):
            p = 6 * i + j
            flat_ref[3 * p:3 * p + 3, :] = filt_ref[i, j].astype(F32)
    rows_i = lax.broadcasted_iota(jnp.int32, (1536, 128), 0)
    cols_i = lax.broadcasted_iota(jnp.int32, (1536, 128), 1)
    d = rows_i // 256
    di = d // 3
    dj = d - 3 * di
    r = rows_i % 256 // 32 - 2 * di
    c = rows_i % 32 - 6 * dj
    ok = (r >= 0) & (r < 6) & (c >= 0) & (c < 18)
    spread = jnp.where(ok & (cols_i == r * 18 + c), 1.0, 0.0).astype(BF)
    for nc in range(4):
        w_ref[nc] = dot(spread, flat_ref[:, nc * 256:(nc + 1) * 256].astype(BF)).astype(BF)

    lanes = lax.broadcasted_iota(jnp.int32, (ROWS, 128), 1)
    subs = lax.broadcasted_iota(jnp.int32, (ROWS, 128), 0)
    rows = jnp.broadcast_to(rows_ref[...], (128, 128)).astype(F32).T[:ROWS]
    hit = rows.astype(jnp.int32) == lanes
    used = jnp.max(jnp.where(hit, 1.0, 0.0), axis=0, keepdims=True)
    low = lax.broadcasted_iota(jnp.int32, (128, 128), 0)
    high = lax.broadcasted_iota(jnp.int32, (128, 128), 1)
    upto = jnp.where(low <= high, 1.0, 0.0).astype(BF)
    rank = dot(jnp.broadcast_to(used, (16, 128)).astype(BF), upto)[0:1] - 1.0
    rank = rank.astype(jnp.int32)
    compact = jnp.where((subs == rank) & (used > 0.0), 1.0, 0.0).astype(BF)
    sel_ref[:, :ROWS] = dot(jnp.where(hit, 1.0, 0.0).astype(BF), compact, (((1,), (1,)), ((), ()))).astype(BF)
    sel_ref[:, ROWS:] = jnp.zeros((ROWS, 256 - ROWS), BF)
    total = jnp.sum(used).astype(jnp.int32)
    nblk_ref[0, 0] = (total + BLK - 1) // BLK
    label = jnp.sum(jnp.where(hit, labels_ref[...], 0), axis=1, keepdims=True)
    coarse = label // 8
    fine = label - coarse * 8
    lab_ref[...] = jnp.where(lanes == 0, coarse, jnp.where(lanes == 1, fine, 0)).astype(BF)
    take = compact[:, :ROWS]
    col = lax.broadcasted_iota(jnp.int32, (1, 1280), 1)
    within = col % 32
    source = (col % 128) // 32 * 192 + 18 * (col // 128) + within
    source = jnp.where(within < 30, source, -1)
    place = lax.broadcasted_iota(jnp.int32, (768, 1280), 0)
    pick_ref[...] = jnp.where(place == source, 1.0, 0.0).astype(BF)
    fetch.wait()
    for part in range(16):
        x_ref[part * ROWS:(part + 1) * ROWS, :] = dot(take, img_ref[:, part * 768:(part + 1) * 768]).astype(BF)

    @pl.loop(0, 5)
    def _(n):
        tile = dot(x_ref[...], pick_ref[:, pl.ds(pl.multiple_of(n * 256, 256), 256)]).astype(BF)
        for h in range(2):
            at = pl.multiple_of((2 * n + h) * 16, 16)
            for part in range(16):
                for b in range(NBLK):
                    row = part * ROWS + b * 16
                    win_ref[part, b, pl.ds(at, 16), :] = tile[row:row + 16, h * 128:(h + 1) * 128]


def prep(images, row_list, labels, filters):
    vmem = pl.BlockSpec(memory_space=pltpu.VMEM)
    return pl.pallas_call(
        prep_kernel,
        out_shape=(
            jax.ShapeDtypeStruct((16, NBLK, 160, 128), BF),
            jax.ShapeDtypeStruct((4, 1536, 256), BF),
            jax.ShapeDtypeStruct((ROWS, 256), BF),
            jax.ShapeDtypeStruct((ROWS, 128), BF),
            jax.ShapeDtypeStruct((1, 1), jnp.int32),
        ),
        in_specs=[vmem, vmem, vmem, pl.BlockSpec(memory_space=pl.ANY)],
        out_specs=(vmem, vmem, vmem, vmem, pl.BlockSpec(memory_space=pltpu.SMEM)),
        scratch_shapes=[
            pltpu.VMEM((ROWS, 12288), BF),
            pltpu.VMEM((16 * ROWS, 768), BF),
            pltpu.VMEM((768, 1280), BF),
            pltpu.VMEM((128, 1024), F32),
            pltpu.SemaphoreType.DMA,
        ],
        compiler_params=pltpu.CompilerParams(vmem_limit_bytes=40 * 2**20),
        name="prep",
    )(jnp.pad(row_list, (0, 32)).reshape(1, 128), jnp.pad(labels, (0, 32)).reshape(1, 128), filters, images)


def conv_kernel(first, count, nblk_ref, win_ref, w_ref, sel_ref, bias_ref, lab_ref, *refs):
    out_ref, uniq_ref = refs[-2:]
    uniq_ref[...] = jnp.zeros_like(uniq_ref)
    if out_ref.shape[1] > count * 1024:
        out_ref[:, count * 1024:] = lab_ref[...]
    steps = []
    for d in range(6):
        for w in range(15):
            steps.append((d, w, 0 if w <= (7 if d < 3 else 6) else 1))

    def block(nc, b, bias, floor, acc):
        total = [[jnp.zeros((16, 256), F32) for _ in range(2)] for _ in range(2)]

        def take(k):
            qr = steps[k][2]
            for m in range(2):
                got = pltpu.matmul_pop(acc[m][k % 8]).reshape(5, 16, 256)
                total[qr][m] = total[qr][m] + jnp.sum(jnp.maximum(got, floor[None]), axis=0)

        for k, (d, w, _) in enumerate(steps):
            if w == 0:
                for m in range(2):
                    pltpu.matmul_push_rhs(w_ref[first + nc, d * 256:(d + 1) * 256, :], d % 2, m)
            for m in range(2):
                rows = slice(m * 80, (m + 1) * 80)
                lhs = jnp.concatenate([win_ref[w, b, rows, :], win_ref[w + 1, b, rows, :]], axis=1)
                pltpu.matmul_acc_lhs(acc[m][k % 8], lhs, load_staged_rhs=d % 2 if w == 0 else None)
            if k >= LAG:
                take(k - LAG)
        for k in range(len(steps) - LAG, len(steps)):
            take(k)
        at = pl.multiple_of(b * 16, 16)
        for qr in range(2):
            for m in range(2):
                q = 2 * qr + m
                mean = (total[qr][m] + 225.0 * bias) * (1.0 / 225.0)
                uniq_ref[pl.ds(at, 16), q * 256:(q + 1) * 256] = mean.astype(BF)

    def scoped(*accs):
        @pl.loop(0, count)
        def _(nc):
            bias = bias_ref[first + nc]
            floor = jnp.broadcast_to(-bias, (16, 256))

            @pl.loop(0, nblk_ref[0, 0])
            def _(b):
                block(nc, b, bias, floor, (accs[:8], accs[8:16]))

            for m in range(2):
                for qr in range(2):
                    q = 2 * qr + m
                    pltpu.matmul_push_rhs(uniq_ref[:, q * 256:(q + 1) * 256], qr, m)
                    pltpu.matmul_acc_lhs(accs[16 + q], sel_ref[...], load_staged_rhs=qr)
            for q in range(4):
                at = pl.multiple_of(nc * 1024 + q * 256, 256)
                out_ref[:, pl.ds(at, 256)] = pltpu.matmul_pop(accs[16 + q]).astype(BF)

    pl.run_scoped(
        scoped,
        *[pltpu.ACC(m)((80, 256), F32) for m in range(2) for _ in range(8)],
        *[pltpu.ACC(q % 2)((ROWS, 256), F32) for q in range(4)],
    )


def conv(first, count, nblk, win, w, sel, bias, lab, extra, after=()):
    return pl.pallas_call(
        functools.partial(conv_kernel, first, count),
        out_shape=jax.ShapeDtypeStruct((ROWS, count * 1024 + extra), BF),
        in_specs=[pl.BlockSpec(memory_space=pltpu.SMEM)] + [pl.BlockSpec(memory_space=pltpu.VMEM)] * 5
        + [pl.BlockSpec(memory_space=pl.ANY)] * len(after),
        out_specs=pl.BlockSpec(memory_space=pltpu.VMEM),
        scratch_shapes=[pltpu.VMEM((256, 1024), BF)],
        compiler_params=pltpu.CompilerParams(vmem_limit_bytes=40 * 2**20),
        cost_estimate=pl.CostEstimate(flops=count * 2 * 86400 * 256 * 256, bytes_accessed=8 * 2**20, transcendentals=0),
        name="conv",
    )(nblk, win, w, sel, bias, lab, *after)


TILES = 16
OWNED = 20
SLOTS = 25
NOTE = 4
FIRST = 5
NTILES = 136
GROUP = 1536
CLASSES = 1000
FEAT = 8


COMMON = tuple((96 * k, 96) for k in range(8)) + ((768, 384),)
BLOCKS = (COMMON + ((1152, 288), (1440, 96)), COMMON + tuple((1152 + 96 * k, 96) for k in range(4)))
COUNT = len(BLOCKS[0]) + len(BLOCKS[1])


def gram_kernel(me_ref, owner_ref, *refs):
    n = len(BLOCKS[0])
    parts, (out_ref, peak_ref) = (refs[:n], refs[n:COUNT]), refs[COUNT:COUNT + 2]
    fa_ref, fb_ref, ft_ref, target_ref, left_ref, list_i, list_j, sem = refs[COUNT + 2:]
    held = (fa_ref, fb_ref)
    me_tile = me_ref[0]
    copies = [
        [
            pltpu.make_async_copy(ref, held[part].at[start:start + size], sem.at[part * n + k])
            for k, (ref, (start, size)) in enumerate(zip(parts[part], BLOCKS[part]))
        ]
        for part in range(2)
    ]
    for group in copies:
        for copy in group:
            copy.start()

    def scan(k, carry):
        i, j, n = carry
        mine = owner_ref[k] == me_tile

        @pl.when(mine)
        def _():
            list_i[n] = i
            list_j[n] = j

        wrap = j == TILES - 1
        i2 = jnp.where(wrap, i + 1, i)
        return i2, jnp.where(wrap, i2, j + 1), n + mine.astype(jnp.int32)

    _, _, owned = lax.fori_loop(0, NTILES, scan, (jnp.int32(0), jnp.int32(0), jnp.int32(0)))
    peak_ref[...] = jnp.zeros_like(peak_ref)

    @pl.loop(owned, OWNED)
    def _(slot):
        for k in range(FEAT):
            out_ref[k, slot + FIRST] = jnp.zeros((32, 256), F32)

    for part in range(2):
        for copy in copies[part]:
            copy.wait()
        for local in range(2):
            for q in range(4):
                cols = slice(local * 1024 + q * 256, local * 1024 + (q + 1) * 256)
                ft_ref[q * 4 + part * 2 + local] = held[part][:, cols].T
    digit = lax.broadcasted_iota(jnp.int32, (128, 256), 0)
    weight = jnp.where(digit == 0, 8.0, jnp.where(digit == 1, 1.0, 0.0)).astype(BF)
    label = dot(fa_ref[:, 2048:], weight)
    classes = lax.broadcasted_iota(jnp.int32, (GROUP, 256), 1).astype(F32)
    for s in range(4):
        target_ref[:, s * 256:(s + 1) * 256] = jnp.where(label == classes + 256.0 * s, 1.0, -1.0).astype(BF)

    def put(slot, product):
        peak_ref[...] = jnp.maximum(peak_ref[...], jnp.max(jnp.abs(product).reshape(32, 8, 256), axis=0))
        for k in range(FEAT):
            out_ref[k, slot] = product[k * 32:(k + 1) * 32, :]

    start = pl.multiple_of(me_tile % 8 * 32, 32)
    for f in range(FEAT):
        t = f // 2 * 4 + f % 2 * 2 + me_tile // 8
        left_ref[f * 32:(f + 1) * 32, :] = ft_ref[t, pl.ds(start, 32), :]
    for s in range(4):
        put(s, dot(left_ref[...], target_ref[:, s * 256:(s + 1) * 256]))
    for s in range(0, FEAT, 2):
        out_ref[s:s + 2, NOTE] = jnp.zeros((2, 32, 256), F32)

    @pl.loop(0, owned)
    def _(slot):
        j = list_j[slot]
        at = pl.multiple_of(j % 2 * 1024 + j // 4 * 256, 256)
        second = j % 4 >= 2

        @pl.when(second)
        def _():
            put(slot + FIRST, dot(ft_ref[list_i[slot]], fb_ref[:, pl.ds(at, 256)]))

        @pl.when(jnp.logical_not(second))
        def _():
            put(slot + FIRST, dot(ft_ref[list_i[slot]], fa_ref[:, pl.ds(at, 256)]))


def gram(me, tile_owner, parts):
    smem = pl.BlockSpec(memory_space=pltpu.SMEM)
    vmem = pl.BlockSpec(memory_space=pltpu.VMEM)
    return pl.pallas_call(
        gram_kernel,
        out_shape=(jax.ShapeDtypeStruct((FEAT, SLOTS, 32, 256), F32), jax.ShapeDtypeStruct((8, 256), F32)),
        in_specs=[smem, smem] + [pl.BlockSpec(memory_space=pltpu.HBM)] * COUNT,
        out_specs=(vmem, vmem),
        scratch_shapes=[
            pltpu.VMEM((GROUP, 2176), BF),
            pltpu.VMEM((GROUP, 2048), BF),
            pltpu.VMEM((TILES, 256, GROUP), BF),
            pltpu.VMEM((GROUP, 1024), BF),
            pltpu.VMEM((256, GROUP), BF),
            pltpu.SMEM((OWNED,), jnp.int32),
            pltpu.SMEM((OWNED,), jnp.int32),
            pltpu.SemaphoreType.DMA((COUNT,)),
        ],
        compiler_params=pltpu.CompilerParams(vmem_limit_bytes=56 * 2**20),
        cost_estimate=pl.CostEstimate(flops=5 * 10**9, bytes_accessed=20 * 2**20, transcendentals=0),
        name="gram",
    )(me, tile_owner, *parts[0], *parts[1])


HALF = jnp.float16


STEPS = (8, 12, 20)


def exchange(partial, peak, owned):
    exponent = jnp.floor(jnp.log2(jnp.maximum(jnp.max(peak), 1e-30)))
    scale = jnp.exp2(13.0 - exponent)

    def some(count, partial):
        used = partial[:, :FIRST + count]
        note = lax.broadcasted_iota(jnp.int32, used.shape, 1) == NOTE
        coded = jnp.where(note, exponent, used * scale).astype(HALF)
        got = lax.all_to_all(coded, "feat", split_axis=0, concat_axis=0, tiled=True)
        back = jnp.exp2(got[:, NOTE:FIRST, :1, :1].astype(F32) - 13.0) * (1.0 / 12288.0)
        total = jnp.sum(got.astype(F32) * back, axis=0)
        cross = total[:NOTE].transpose(1, 0, 2).reshape(32, 1024)[:, :CLASSES]
        return jnp.pad(total[FIRST:], ((0, OWNED - count), (0, 0), (0, 0))), cross

    level = sum((owned > step).astype(jnp.int32) for step in STEPS[:-1])
    return lax.switch(level, [functools.partial(some, step) for step in STEPS], partial)


def hop(dy=0, dx=0, core=0):
    def index(y, x, c):
        return (y % 2 * 4 + x % 4) * 2 + c % 2

    return [(index(y, x, c), index(y + dy, x + dx, c + core)) for y in range(2) for x in range(4) for c in range(2)]


def onward():
    return [(s, d) if s % 2 == 0 else (s, e) for (s, d), (_, e) in zip(hop(dx=1), hop(dx=-1))]


def send(block, perm):
    return lax.ppermute(block, "tile", perm)


def spread_first(own):
    left = send(own, hop(dx=1))
    right = send(own, hop(dx=-1))
    over = send(own, hop(dy=1))
    return own, over, left, right


def spread_second(first, earlier=None):
    own, over, left, right = first
    even = lax.axis_index("tile") % 2 == 0
    far = send(jnp.where(even, left, right), onward())
    if earlier is not None:
        over, far, *earlier[7:10] = lax.optimization_barrier((over, far, *earlier[7:10]))
    over_left = send(over, hop(dx=1))
    over_right = send(over, hop(dx=-1))
    swap_a = send(jnp.concatenate([own, over, left, right], axis=0), hop(core=1))
    return far, over_left, over_right, swap_a


def spread_third(first, second, apart):
    own, over, left, right = first
    far, over_left, over_right, swap_a = second
    over_far = send(far, hop(dy=1))
    held = [own, over, left, right, over_left, over_right, far, over_far, swap_a]
    if apart:
        far_swap = send(far, hop(core=1))
        rest = lax.optimization_barrier((over_left, over_right, over_far))
        swaps = [send(block, hop(core=1)) for block in rest]
        return held + [swaps[0], swaps[1], far_swap, swaps[2]]
    swap_b = send(jnp.concatenate([over_left, over_right, far], axis=0), hop(core=1))
    return held + [swap_b, send(over_far, hop(core=1))]


def body(images, row_list, labels, filters, bias, tile_owner):
    win, w, sel, lab, nblk = prep(images, row_list, labels, filters)
    bias4 = bias.reshape(4, 1, 256)
    own_a = conv(0, 2, nblk, win, w, sel, bias4, lab, 128)
    first_a = spread_first(own_a)
    own_b2 = conv(2, 1, nblk, win, w, sel, bias4, lab, 0, (own_a,))
    second_a = spread_second(first_a)
    own_b3 = conv(3, 1, nblk, win, w, sel, bias4, lab, 0, first_a[1:])
    own_b = jnp.concatenate([own_b2, own_b3], axis=1)
    own_b, far, over_left, over_right = lax.optimization_barrier((own_b,) + second_a[:3])
    second_a = (far, over_left, over_right, second_a[3])
    first_b = spread_first(own_b)
    part_a = spread_third(first_a, second_a, False)
    second_b = spread_second(first_b, part_a)
    part_b = spread_third(first_b, second_b, True)
    me = jnp.stack([lax.axis_index("tile"), lax.axis_index("feat")]).astype(jnp.int32)
    partial, peak = gram(me, tile_owner, (part_a, part_b))
    owned = jnp.sum((tile_owner == me[0]).astype(jnp.int32))
    return exchange(partial, peak, owned)


def solution(mesh):
    def run(*args):
        return jax.shard_map(
            body,
            mesh=mesh,
            in_specs=(P(("feat", "tile"), None), P(("feat", "tile")), P(("feat", "tile")), P(), P(), P()),
            out_specs=(P("tile", "feat", None), P(("feat", "tile"), None)),
            check_vma=False,
        )(*args)

    return run
```

```python
import functools

import jax
import jax.numpy as jnp
from jax import lax
from jax.experimental import pallas as pl
from jax.experimental.pallas import tpu as pltpu
from jax.sharding import PartitionSpec as P

ROWS = 96
BLK = 16
NBLK = 6
WIDE = 112
BF = jnp.bfloat16
F32 = jnp.float32
LAG = 3


def dot(a, b, dims=(((1,), (0,)), ((), ()))):
    return lax.dot_general(a, b, dims, preferred_element_type=F32)


def prep_kernel(rows_ref, labels_ref, filt_ref, img_hbm, win_ref, half_ref, w_ref, sel_ref, lab_ref, nblk_ref, img_ref, x_ref, pick_ref, flat_ref, sem):
    fetch = pltpu.make_async_copy(img_hbm, img_ref, sem)
    fetch.start()
    flat_ref[...] = jnp.zeros_like(flat_ref)
    for i in range(6):
        for j in range(6):
            p = 6 * i + j
            flat_ref[3 * p:3 * p + 3, :] = filt_ref[i, j].astype(F32)
    rows_i = lax.broadcasted_iota(jnp.int32, (1536, 128), 0)
    cols_i = lax.broadcasted_iota(jnp.int32, (1536, 128), 1)
    d = rows_i // 256
    di = d // 3
    dj = d - 3 * di
    r = rows_i % 256 // 32 - 2 * di
    c = rows_i % 32 - 6 * dj
    ok = (r >= 0) & (r < 6) & (c >= 0) & (c < 18)
    spread = jnp.where(ok & (cols_i == r * 18 + c), 1.0, 0.0).astype(BF)
    for nc in range(4):
        w_ref[nc] = dot(spread, flat_ref[:, nc * 256:(nc + 1) * 256].astype(BF)).astype(BF)

    lanes = lax.broadcasted_iota(jnp.int32, (ROWS, 128), 1)
    subs = lax.broadcasted_iota(jnp.int32, (ROWS, 128), 0)
    rows = jnp.broadcast_to(rows_ref[...], (128, 128)).astype(F32).T[:ROWS]
    hit = rows.astype(jnp.int32) == lanes
    used = jnp.max(jnp.where(hit, 1.0, 0.0), axis=0, keepdims=True)
    low = lax.broadcasted_iota(jnp.int32, (128, 128), 0)
    high = lax.broadcasted_iota(jnp.int32, (128, 128), 1)
    upto = jnp.where(low <= high, 1.0, 0.0).astype(BF)
    rank = dot(jnp.broadcast_to(used, (16, 128)).astype(BF), upto)[0:1] - 1.0
    rank = rank.astype(jnp.int32)
    total = jnp.sum(used).astype(jnp.int32)
    whole = (total + 7) // BLK
    nblk_ref[0, 0] = whole
    nblk_ref[0, 1] = total - whole * BLK
    deep = lax.broadcasted_iota(jnp.int32, (WIDE, 128), 0)
    deep = jnp.where(deep < ROWS, deep, jnp.where(deep < ROWS + 8, deep - ROWS + BLK * whole, -1))
    take = jnp.where((deep == rank) & (used > 0.0), 1.0, 0.0).astype(BF)
    compact = take[:ROWS]
    sel_ref[:, :ROWS] = dot(jnp.where(hit, 1.0, 0.0).astype(BF), compact, (((1,), (1,)), ((), ()))).astype(BF)
    sel_ref[:, ROWS:] = jnp.zeros((ROWS, 256 - ROWS), BF)
    label = jnp.sum(jnp.where(hit, labels_ref[...], 0), axis=1, keepdims=True)
    coarse = label // 8
    fine = label - coarse * 8
    lab_ref[...] = jnp.where(lanes == 0, coarse, jnp.where(lanes == 1, fine, 0)).astype(BF)
    col = lax.broadcasted_iota(jnp.int32, (1, 1280), 1)
    within = col % 32
    source = (col % 128) // 32 * 192 + 18 * (col // 128) + within
    source = jnp.where(within < 30, source, -1)
    place = lax.broadcasted_iota(jnp.int32, (768, 1280), 0)
    pick_ref[...] = jnp.where(place == source, 1.0, 0.0).astype(BF)
    fetch.wait()
    for part in range(16):
        x_ref[part * WIDE:(part + 1) * WIDE, :] = dot(take[:, :ROWS], img_ref[:, part * 768:(part + 1) * 768]).astype(BF)

    @pl.loop(0, 5)
    def _(n):
        fine = dot(x_ref[...], pick_ref[:, pl.ds(pl.multiple_of(n * 256, 256), 256)])
        tile = fine.astype(BF)
        for part in range(16):
            row = part * WIDE + ROWS
            pair = jnp.concatenate([fine[row:row + 8, :128], fine[row:row + 8, 128:]], axis=0)
            half_ref[part, pl.ds(pl.multiple_of(n * 16, 16), 16), :] = pair.astype(BF)
        for h in range(2):
            at = pl.multiple_of((2 * n + h) * 16, 16)
            for part in range(16):
                for b in range(NBLK):
                    row = part * WIDE + b * 16
                    win_ref[part, b, pl.ds(at, 16), :] = tile[row:row + 16, h * 128:(h + 1) * 128]


def prep(images, row_list, labels, filters):
    vmem = pl.BlockSpec(memory_space=pltpu.VMEM)
    return pl.pallas_call(
        prep_kernel,
        out_shape=(
            jax.ShapeDtypeStruct((16, NBLK, 160, 128), BF),
            jax.ShapeDtypeStruct((16, 80, 128), BF),
            jax.ShapeDtypeStruct((4, 1536, 256), BF),
            jax.ShapeDtypeStruct((ROWS, 256), BF),
            jax.ShapeDtypeStruct((ROWS, 128), BF),
            jax.ShapeDtypeStruct((1, 2), jnp.int32),
        ),
        in_specs=[vmem, vmem, vmem, pl.BlockSpec(memory_space=pl.ANY)],
        out_specs=(vmem, vmem, vmem, vmem, vmem, pl.BlockSpec(memory_space=pltpu.SMEM)),
        scratch_shapes=[
            pltpu.VMEM((ROWS, 12288), BF),
            pltpu.VMEM((16 * WIDE, 768), BF),
            pltpu.VMEM((768, 1280), BF),
            pltpu.VMEM((128, 1024), F32),
            pltpu.SemaphoreType.DMA,
        ],
        compiler_params=pltpu.CompilerParams(vmem_limit_bytes=40 * 2**20),
        name="prep",
    )(jnp.pad(row_list, (0, 32)).reshape(1, 128), jnp.pad(labels, (0, 32)).reshape(1, 128), filters, images)


def conv_kernel(first, count, nblk_ref, win_ref, half_ref, w_ref, sel_ref, bias_ref, lab_ref, *refs):
    out_ref, uniq_ref = refs[-2:]
    uniq_ref[...] = jnp.zeros_like(uniq_ref)
    if out_ref.shape[1] > count * 1024:
        out_ref[:, count * 1024:] = lab_ref[...]
    steps = []
    for d in range(6):
        for w in range(15):
            steps.append((d, w, 0 if w <= (7 if d < 3 else 6) else 1))

    def block(nc, b, bias, floor, acc):
        total = [[jnp.zeros((16, 256), F32) for _ in range(2)] for _ in range(2)]

        def take(k):
            qr = steps[k][2]
            for m in range(2):
                got = pltpu.matmul_pop(acc[m][k % 8]).reshape(5, 16, 256)
                total[qr][m] = total[qr][m] + jnp.sum(jnp.maximum(got, floor[None]), axis=0)

        for k, (d, w, _) in enumerate(steps):
            if w == 0:
                for m in range(2):
                    pltpu.matmul_push_rhs(w_ref[first + nc, d * 256:(d + 1) * 256, :], d % 2, m)
            for m in range(2):
                rows = slice(m * 80, (m + 1) * 80)
                lhs = jnp.concatenate([win_ref[w, b, rows, :], win_ref[w + 1, b, rows, :]], axis=1)
                pltpu.matmul_acc_lhs(acc[m][k % 8], lhs, load_staged_rhs=d % 2 if w == 0 else None)
            if k >= LAG:
                take(k - LAG)
        for k in range(len(steps) - LAG, len(steps)):
            take(k)
        at = pl.multiple_of(b * 16, 16)
        for qr in range(2):
            for m in range(2):
                q = 2 * qr + m
                mean = (total[qr][m] + 225.0 * bias) * (1.0 / 225.0)
                uniq_ref[pl.ds(at, 16), q * 256:(q + 1) * 256] = mean.astype(BF)

    def half_block(nc, b, bias, floor, acc):
        total = [[jnp.zeros((8, 256), F32) for _ in range(2)] for _ in range(2)]
        low = floor[:8]

        def take(k):
            d, j = k // 8, k % 8
            for m in range(2):
                w = 2 * j + m
                if w < 15:
                    qr = 0 if w <= (7 if d < 3 else 6) else 1
                    got = jnp.maximum(pltpu.matmul_pop(acc[m][k % 8]).reshape(10, 8, 256), low[None])
                    total[qr][0] = total[qr][0] + jnp.sum(got[:5], axis=0)
                    total[qr][1] = total[qr][1] + jnp.sum(got[5:], axis=0)

        for k in range(48):
            d, j = k // 8, k % 8
            if j == 0:
                for m in range(2):
                    pltpu.matmul_push_rhs(w_ref[first + nc, d * 256:(d + 1) * 256, :], d % 2, m)
            for m in range(2):
                w = 2 * j + m
                if w < 15:
                    lhs = jnp.concatenate([half_ref[w], half_ref[w + 1]], axis=1)
                    pltpu.matmul_acc_lhs(acc[m][k % 8], lhs, load_staged_rhs=d % 2 if j == 0 else None)
            if k >= LAG:
                take(k - LAG)
        for k in range(48 - LAG, 48):
            take(k)
        at = pl.multiple_of(b * 16, 16)
        for q in range(4):
            mean = (total[q // 2][q % 2] + 225.0 * bias) * (1.0 / 225.0)
            uniq_ref[pl.ds(at, 16), q * 256:(q + 1) * 256] = jnp.concatenate([mean, jnp.zeros_like(mean)], axis=0).astype(BF)

    def scoped(*accs):
        @pl.loop(0, count)
        def _(nc):
            bias = bias_ref[first + nc]
            floor = jnp.broadcast_to(-bias, (16, 256))

            @pl.loop(0, nblk_ref[0, 0])
            def _(b):
                block(nc, b, bias, floor, (accs[:8], accs[8:16]))

            @pl.when(nblk_ref[0, 1] > 0)
            def _():
                half_block(nc, nblk_ref[0, 0], bias, floor, (accs[:8], accs[8:16]))

            for m in range(2):
                for qr in range(2):
                    q = 2 * qr + m
                    pltpu.matmul_push_rhs(uniq_ref[:, q * 256:(q + 1) * 256], qr, m)
                    pltpu.matmul_acc_lhs(accs[16 + q], sel_ref[...], load_staged_rhs=qr)
            for q in range(4):
                at = pl.multiple_of(nc * 1024 + q * 256, 256)
                out_ref[:, pl.ds(at, 256)] = pltpu.matmul_pop(accs[16 + q]).astype(BF)

    pl.run_scoped(
        scoped,
        *[pltpu.ACC(m)((80, 256), F32) for m in range(2) for _ in range(8)],
        *[pltpu.ACC(q % 2)((ROWS, 256), F32) for q in range(4)],
    )


def conv(first, count, nblk, win, half, w, sel, bias, lab, extra, after=()):
    return pl.pallas_call(
        functools.partial(conv_kernel, first, count),
        out_shape=jax.ShapeDtypeStruct((ROWS, count * 1024 + extra), BF),
        in_specs=[pl.BlockSpec(memory_space=pltpu.SMEM)] + [pl.BlockSpec(memory_space=pltpu.VMEM)] * 6
        + [pl.BlockSpec(memory_space=pl.ANY)] * len(after),
        out_specs=pl.BlockSpec(memory_space=pltpu.VMEM),
        scratch_shapes=[pltpu.VMEM((256, 1024), BF)],
        compiler_params=pltpu.CompilerParams(vmem_limit_bytes=40 * 2**20),
        cost_estimate=pl.CostEstimate(flops=count * 2 * 86400 * 256 * 256, bytes_accessed=8 * 2**20, transcendentals=0),
        name="conv",
    )(nblk, win, half, w, sel, bias, lab, *after)


TILES = 16
OWNED = 20
SLOTS = 25
NOTE = 4
FIRST = 5
NTILES = 136
GROUP = 1536
CLASSES = 1000
FEAT = 8


BLOCKS = ((0, 96), (96, 96), (192, 96), (288, 96), (384, 96), (480, 96), (576, 96), (672, 96), (768, 384), (1152, 288), (1440, 96))


def gram_kernel(me_ref, owner_ref, *refs):
    n = len(BLOCKS)
    parts, (out_ref, peak_ref) = (refs[:n], refs[n:2 * n]), refs[2 * n:2 * n + 2]
    fa_ref, fb_ref, ft_ref, target_ref, left_ref, list_i, list_j, sem = refs[2 * n + 2:]
    held = (fa_ref, fb_ref)
    me_tile = me_ref[0]
    copies = [
        [
            pltpu.make_async_copy(ref, held[part].at[start:start + size], sem.at[part * n + k])
            for k, (ref, (start, size)) in enumerate(zip(parts[part], BLOCKS))
        ]
        for part in range(2)
    ]
    for group in copies:
        for copy in group:
            copy.start()

    def scan(k, carry):
        i, j, n = carry
        mine = owner_ref[k] == me_tile

        @pl.when(mine)
        def _():
            list_i[n] = i
            list_j[n] = j

        wrap = j == TILES - 1
        i2 = jnp.where(wrap, i + 1, i)
        return i2, jnp.where(wrap, i2, j + 1), n + mine.astype(jnp.int32)

    _, _, owned = lax.fori_loop(0, NTILES, scan, (jnp.int32(0), jnp.int32(0), jnp.int32(0)))
    peak_ref[...] = jnp.zeros_like(peak_ref)

    @pl.loop(owned, OWNED)
    def _(slot):
        for k in range(FEAT):
            out_ref[k, slot + FIRST] = jnp.zeros((32, 256), F32)

    for part in range(2):
        for copy in copies[part]:
            copy.wait()
        for local in range(2):
            for q in range(4):
                cols = slice(local * 1024 + q * 256, local * 1024 + (q + 1) * 256)
                ft_ref[q * 4 + part * 2 + local] = held[part][:, cols].T
    digit = lax.broadcasted_iota(jnp.int32, (128, 256), 0)
    weight = jnp.where(digit == 0, 8.0, jnp.where(digit == 1, 1.0, 0.0)).astype(BF)
    label = dot(fa_ref[:, 2048:], weight)
    classes = lax.broadcasted_iota(jnp.int32, (GROUP, 256), 1).astype(F32)
    for s in range(4):
        target_ref[:, s * 256:(s + 1) * 256] = jnp.where(label == classes + 256.0 * s, 1.0, -1.0).astype(BF)

    def put(slot, product):
        peak_ref[...] = jnp.maximum(peak_ref[...], jnp.max(jnp.abs(product).reshape(32, 8, 256), axis=0))
        for k in range(FEAT):
            out_ref[k, slot] = product[k * 32:(k + 1) * 32, :]

    start = pl.multiple_of(me_tile % 8 * 32, 32)
    for f in range(FEAT):
        t = f // 2 * 4 + f % 2 * 2 + me_tile // 8
        left_ref[f * 32:(f + 1) * 32, :] = ft_ref[t, pl.ds(start, 32), :]
    for s in range(4):
        put(s, dot(left_ref[...], target_ref[:, s * 256:(s + 1) * 256]))
    for s in range(0, FEAT, 2):
        out_ref[s:s + 2, NOTE] = jnp.zeros((2, 32, 256), F32)

    @pl.loop(0, owned)
    def _(slot):
        j = list_j[slot]
        at = pl.multiple_of(j % 2 * 1024 + j // 4 * 256, 256)
        second = j % 4 >= 2

        @pl.when(second)
        def _():
            put(slot + FIRST, dot(ft_ref[list_i[slot]], fb_ref[:, pl.ds(at, 256)]))

        @pl.when(jnp.logical_not(second))
        def _():
            put(slot + FIRST, dot(ft_ref[list_i[slot]], fa_ref[:, pl.ds(at, 256)]))


def gram(me, tile_owner, parts):
    smem = pl.BlockSpec(memory_space=pltpu.SMEM)
    vmem = pl.BlockSpec(memory_space=pltpu.VMEM)
    return pl.pallas_call(
        gram_kernel,
        out_shape=(jax.ShapeDtypeStruct((FEAT, SLOTS, 32, 256), F32), jax.ShapeDtypeStruct((8, 256), F32)),
        in_specs=[smem, smem] + [pl.BlockSpec(memory_space=pltpu.HBM)] * (2 * len(BLOCKS)),
        out_specs=(vmem, vmem),
        scratch_shapes=[
            pltpu.VMEM((GROUP, 2176), BF),
            pltpu.VMEM((GROUP, 2048), BF),
            pltpu.VMEM((TILES, 256, GROUP), BF),
            pltpu.VMEM((GROUP, 1024), BF),
            pltpu.VMEM((256, GROUP), BF),
            pltpu.SMEM((OWNED,), jnp.int32),
            pltpu.SMEM((OWNED,), jnp.int32),
            pltpu.SemaphoreType.DMA((2 * len(BLOCKS),)),
        ],
        compiler_params=pltpu.CompilerParams(vmem_limit_bytes=56 * 2**20),
        cost_estimate=pl.CostEstimate(flops=5 * 10**9, bytes_accessed=20 * 2**20, transcendentals=0),
        name="gram",
    )(me, tile_owner, *parts[0], *parts[1])


HALF = jnp.float16


STEPS = (8, 12, 20)


def exchange(partial, peak, owned):
    exponent = jnp.floor(jnp.log2(jnp.maximum(jnp.max(peak), 1e-30)))
    scale = jnp.exp2(13.0 - exponent)

    def some(count, partial):
        used = partial[:, :FIRST + count]
        note = lax.broadcasted_iota(jnp.int32, used.shape, 1) == NOTE
        coded = jnp.where(note, exponent, used * scale).astype(HALF)
        got = lax.all_to_all(coded, "feat", split_axis=0, concat_axis=0, tiled=True)
        back = jnp.exp2(got[:, NOTE:FIRST, :1, :1].astype(F32) - 13.0) * (1.0 / 12288.0)
        total = jnp.sum(got.astype(F32) * back, axis=0)
        cross = total[:NOTE].transpose(1, 0, 2).reshape(32, 1024)[:, :CLASSES]
        return jnp.pad(total[FIRST:], ((0, OWNED - count), (0, 0), (0, 0))), cross

    level = sum((owned > step).astype(jnp.int32) for step in STEPS[:-1])
    return lax.switch(level, [functools.partial(some, step) for step in STEPS], partial)


def hop(dy=0, dx=0, core=0):
    def index(y, x, c):
        return (y % 2 * 4 + x % 4) * 2 + c % 2

    return [(index(y, x, c), index(y + dy, x + dx, c + core)) for y in range(2) for x in range(4) for c in range(2)]


def onward():
    return [(s, d) if s % 2 == 0 else (s, e) for (s, d), (_, e) in zip(hop(dx=1), hop(dx=-1))]


def send(block, perm):
    return lax.ppermute(block, "tile", perm)


def spread_first(own):
    left = send(own, hop(dx=1))
    right = send(own, hop(dx=-1))
    over = send(own, hop(dy=1))
    return own, over, left, right


def spread_second(first):
    own, over, left, right = first
    even = lax.axis_index("tile") % 2 == 0
    far = send(jnp.where(even, left, right), onward())
    over_left = send(over, hop(dx=1))
    over_right = send(over, hop(dx=-1))
    swap_a = send(jnp.concatenate([own, over, left, right], axis=0), hop(core=1))
    return far, over_left, over_right, swap_a


def spread_third(first, second):
    own, over, left, right = first
    far, over_left, over_right, swap_a = second
    even = lax.axis_index("tile") % 2 == 0
    over_far = send(jnp.where(even, over_left, over_right), onward())
    swap_b = send(jnp.concatenate([over_left, over_right, far], axis=0), hop(core=1))
    swap_c = send(over_far, hop(core=1))
    return [own, over, left, right, over_left, over_right, far, over_far, swap_a, swap_b, swap_c]


def body(images, row_list, labels, filters, bias, tile_owner):
    win, half, w, sel, lab, nblk = prep(images, row_list, labels, filters)
    bias4 = bias.reshape(4, 1, 256)
    own_a = conv(0, 2, nblk, win, half, w, sel, bias4, lab, 128)
    first_a = spread_first(own_a)
    own_b2 = conv(2, 1, nblk, win, half, w, sel, bias4, lab, 0, (own_a,))
    second_a = spread_second(first_a)
    own_b3 = conv(3, 1, nblk, win, half, w, sel, bias4, lab, 0, first_a[1:])
    own_b = jnp.concatenate([own_b2, own_b3], axis=1)
    own_b, far, over_left, over_right = lax.optimization_barrier((own_b,) + second_a[:3])
    second_a = (far, over_left, over_right, second_a[3])
    first_b = spread_first(own_b)
    part_a = spread_third(first_a, second_a)
    second_b = spread_second(first_b)
    part_b = spread_third(first_b, second_b)
    me = jnp.stack([lax.axis_index("tile"), lax.axis_index("feat")]).astype(jnp.int32)
    partial, peak = gram(me, tile_owner, (part_a, part_b))
    owned = jnp.sum((tile_owner == me[0]).astype(jnp.int32))
    return exchange(partial, peak, owned)


def solution(mesh):
    def run(*args):
        return jax.shard_map(
            body,
            mesh=mesh,
            in_specs=(P(("feat", "tile"), None), P(("feat", "tile")), P(("feat", "tile")), P(), P(), P()),
            out_specs=(P("tile", "feat", None), P(("feat", "tile"), None)),
            check_vma=False,
        )(*args)

    return run
```

```python
import functools

import jax
import jax.numpy as jnp
from jax import lax
from jax.experimental import pallas as pl
from jax.experimental.pallas import tpu as pltpu
from jax.sharding import PartitionSpec as P

ROWS = 96
BLK = 16
NBLK = 6
WIDE = 112
BF = jnp.bfloat16
F32 = jnp.float32
LAG = 3


def dot(a, b, dims=(((1,), (0,)), ((), ()))):
    return lax.dot_general(a, b, dims, preferred_element_type=F32)


def prep_kernel(rows_ref, labels_ref, filt_ref, img_hbm, win_ref, half_ref, w_ref, sel_ref, lab_ref, nblk_ref, img_ref, x_ref, pick_ref, flat_ref, sem):
    fetch = pltpu.make_async_copy(img_hbm, img_ref, sem)
    fetch.start()
    flat_ref[...] = jnp.zeros_like(flat_ref)
    for i in range(6):
        for j in range(6):
            p = 6 * i + j
            flat_ref[3 * p:3 * p + 3, :] = filt_ref[i, j].astype(F32)
    rows_i = lax.broadcasted_iota(jnp.int32, (1536, 128), 0)
    cols_i = lax.broadcasted_iota(jnp.int32, (1536, 128), 1)
    d = rows_i // 256
    di = d // 3
    dj = d - 3 * di
    r = rows_i % 256 // 32 - 2 * di
    c = rows_i % 32 - 6 * dj
    ok = (r >= 0) & (r < 6) & (c >= 0) & (c < 18)
    spread = jnp.where(ok & (cols_i == r * 18 + c), 1.0, 0.0).astype(BF)
    for nc in range(4):
        w_ref[nc] = dot(spread, flat_ref[:, nc * 256:(nc + 1) * 256].astype(BF)).astype(BF)

    lanes = lax.broadcasted_iota(jnp.int32, (ROWS, 128), 1)
    subs = lax.broadcasted_iota(jnp.int32, (ROWS, 128), 0)
    rows = jnp.broadcast_to(rows_ref[...], (128, 128)).astype(F32).T[:ROWS]
    hit = rows.astype(jnp.int32) == lanes
    used = jnp.max(jnp.where(hit, 1.0, 0.0), axis=0, keepdims=True)
    low = lax.broadcasted_iota(jnp.int32, (128, 128), 0)
    high = lax.broadcasted_iota(jnp.int32, (128, 128), 1)
    upto = jnp.where(low <= high, 1.0, 0.0).astype(BF)
    rank = dot(jnp.broadcast_to(used, (16, 128)).astype(BF), upto)[0:1] - 1.0
    rank = rank.astype(jnp.int32)
    total = jnp.sum(used).astype(jnp.int32)
    whole = (total + 7) // BLK
    nblk_ref[0, 0] = whole
    nblk_ref[0, 1] = total - whole * BLK
    deep = lax.broadcasted_iota(jnp.int32, (WIDE, 128), 0)
    deep = jnp.where(deep < ROWS, deep, jnp.where(deep < ROWS + 8, deep - ROWS + BLK * whole, -1))
    take = jnp.where((deep == rank) & (used > 0.0), 1.0, 0.0).astype(BF)
    compact = take[:ROWS]
    sel_ref[:, :ROWS] = dot(jnp.where(hit, 1.0, 0.0).astype(BF), compact, (((1,), (1,)), ((), ()))).astype(BF)
    sel_ref[:, ROWS:] = jnp.zeros((ROWS, 256 - ROWS), BF)
    label = jnp.sum(jnp.where(hit, labels_ref[...], 0), axis=1, keepdims=True)
    coarse = label // 8
    fine = label - coarse * 8
    lab_ref[...] = jnp.where(lanes == 0, coarse, jnp.where(lanes == 1, fine, 0)).astype(BF)
    col = lax.broadcasted_iota(jnp.int32, (1, 1280), 1)
    within = col % 32
    source = (col % 128) // 32 * 192 + 18 * (col // 128) + within
    source = jnp.where(within < 30, source, -1)
    place = lax.broadcasted_iota(jnp.int32, (768, 1280), 0)
    pick_ref[...] = jnp.where(place == source, 1.0, 0.0).astype(BF)
    fetch.wait()
    for part in range(16):
        x_ref[part * WIDE:(part + 1) * WIDE, :] = dot(take[:, :ROWS], img_ref[:, part * 768:(part + 1) * 768]).astype(BF)

    @pl.loop(0, 5)
    def _(n):
        fine = dot(x_ref[...], pick_ref[:, pl.ds(pl.multiple_of(n * 256, 256), 256)])
        tile = fine.astype(BF)
        for part in range(16):
            row = part * WIDE + ROWS
            pair = jnp.concatenate([fine[row:row + 8, :128], fine[row:row + 8, 128:]], axis=0)
            half_ref[part, pl.ds(pl.multiple_of(n * 16, 16), 16), :] = pair.astype(BF)
        for h in range(2):
            at = pl.multiple_of((2 * n + h) * 16, 16)
            for part in range(16):
                for b in range(NBLK):
                    row = part * WIDE + b * 16
                    win_ref[part, b, pl.ds(at, 16), :] = tile[row:row + 16, h * 128:(h + 1) * 128]


def prep(images, row_list, labels, filters):
    vmem = pl.BlockSpec(memory_space=pltpu.VMEM)
    return pl.pallas_call(
        prep_kernel,
        out_shape=(
            jax.ShapeDtypeStruct((16, NBLK, 160, 128), BF),
            jax.ShapeDtypeStruct((16, 80, 128), BF),
            jax.ShapeDtypeStruct((4, 1536, 256), BF),
            jax.ShapeDtypeStruct((ROWS, 256), BF),
            jax.ShapeDtypeStruct((ROWS, 128), BF),
            jax.ShapeDtypeStruct((1, 2), jnp.int32),
        ),
        in_specs=[vmem, vmem, vmem, pl.BlockSpec(memory_space=pl.ANY)],
        out_specs=(vmem, vmem, vmem, vmem, vmem, pl.BlockSpec(memory_space=pltpu.SMEM)),
        scratch_shapes=[
            pltpu.VMEM((ROWS, 12288), BF),
            pltpu.VMEM((16 * WIDE, 768), BF),
            pltpu.VMEM((768, 1280), BF),
            pltpu.VMEM((128, 1024), F32),
            pltpu.SemaphoreType.DMA,
        ],
        compiler_params=pltpu.CompilerParams(vmem_limit_bytes=40 * 2**20),
        name="prep",
    )(jnp.pad(row_list, (0, 32)).reshape(1, 128), jnp.pad(labels, (0, 32)).reshape(1, 128), filters, images)


def conv_kernel(first, count, nblk_ref, win_ref, half_ref, w_ref, sel_ref, bias_ref, lab_ref, *refs):
    out_ref, uniq_ref = refs[-2:]
    uniq_ref[...] = jnp.zeros_like(uniq_ref)
    if out_ref.shape[1] > count * 1024:
        out_ref[:, count * 1024:] = lab_ref[...]
    steps = []
    for d in range(6):
        for w in range(15):
            steps.append((d, w, 0 if w <= (7 if d < 3 else 6) else 1))

    def block(nc, b, bias, floor, acc):
        total = [[jnp.zeros((16, 256), F32) for _ in range(2)] for _ in range(2)]

        def take(k):
            qr = steps[k][2]
            for m in range(2):
                got = pltpu.matmul_pop(acc[m][k % 8]).reshape(5, 16, 256)
                total[qr][m] = total[qr][m] + jnp.sum(jnp.maximum(got, floor[None]), axis=0)

        for k, (d, w, _) in enumerate(steps):
            if w == 0:
                for m in range(2):
                    pltpu.matmul_push_rhs(w_ref[first + nc, d * 256:(d + 1) * 256, :], d % 2, m)
            for m in range(2):
                rows = slice(m * 80, (m + 1) * 80)
                lhs = jnp.concatenate([win_ref[w, b, rows, :], win_ref[w + 1, b, rows, :]], axis=1)
                pltpu.matmul_acc_lhs(acc[m][k % 8], lhs, load_staged_rhs=d % 2 if w == 0 else None)
            if k >= LAG:
                take(k - LAG)
        for k in range(len(steps) - LAG, len(steps)):
            take(k)
        at = pl.multiple_of(b * 16, 16)
        for qr in range(2):
            for m in range(2):
                q = 2 * qr + m
                mean = (total[qr][m] + 225.0 * bias) * (1.0 / 225.0)
                uniq_ref[pl.ds(at, 16), q * 256:(q + 1) * 256] = mean.astype(BF)

    def half_block(nc, b, bias, floor, acc):
        total = [[jnp.zeros((8, 256), F32) for _ in range(2)] for _ in range(2)]
        low = floor[:8]

        def take(k):
            d, j = k // 8, k % 8
            for m in range(2):
                w = 2 * j + m
                if w < 15:
                    qr = 0 if w <= (7 if d < 3 else 6) else 1
                    got = jnp.maximum(pltpu.matmul_pop(acc[m][k % 8]).reshape(10, 8, 256), low[None])
                    total[qr][0] = total[qr][0] + jnp.sum(got[:5], axis=0)
                    total[qr][1] = total[qr][1] + jnp.sum(got[5:], axis=0)

        for k in range(48):
            d, j = k // 8, k % 8
            if j == 0:
                for m in range(2):
                    pltpu.matmul_push_rhs(w_ref[first + nc, d * 256:(d + 1) * 256, :], d % 2, m)
            for m in range(2):
                w = 2 * j + m
                if w < 15:
                    lhs = jnp.concatenate([half_ref[w], half_ref[w + 1]], axis=1)
                    pltpu.matmul_acc_lhs(acc[m][k % 8], lhs, load_staged_rhs=d % 2 if j == 0 else None)
            if k >= LAG:
                take(k - LAG)
        for k in range(48 - LAG, 48):
            take(k)
        at = pl.multiple_of(b * 16, 16)
        for q in range(4):
            mean = (total[q // 2][q % 2] + 225.0 * bias) * (1.0 / 225.0)
            uniq_ref[pl.ds(at, 16), q * 256:(q + 1) * 256] = jnp.concatenate([mean, jnp.zeros_like(mean)], axis=0).astype(BF)

    def scoped(*accs):
        @pl.loop(0, count)
        def _(nc):
            bias = bias_ref[first + nc]
            floor = jnp.broadcast_to(-bias, (16, 256))

            @pl.loop(0, nblk_ref[0, 0])
            def _(b):
                block(nc, b, bias, floor, (accs[:8], accs[8:16]))

            @pl.when(nblk_ref[0, 1] > 0)
            def _():
                half_block(nc, nblk_ref[0, 0], bias, floor, (accs[:8], accs[8:16]))

            for m in range(2):
                for qr in range(2):
                    q = 2 * qr + m
                    pltpu.matmul_push_rhs(uniq_ref[:, q * 256:(q + 1) * 256], qr, m)
                    pltpu.matmul_acc_lhs(accs[16 + q], sel_ref[...], load_staged_rhs=qr)
            for q in range(4):
                at = pl.multiple_of(nc * 1024 + q * 256, 256)
                out_ref[:, pl.ds(at, 256)] = pltpu.matmul_pop(accs[16 + q]).astype(BF)

    pl.run_scoped(
        scoped,
        *[pltpu.ACC(m)((80, 256), F32) for m in range(2) for _ in range(8)],
        *[pltpu.ACC(q % 2)((ROWS, 256), F32) for q in range(4)],
    )


def conv(first, count, nblk, win, half, w, sel, bias, lab, extra, after=()):
    return pl.pallas_call(
        functools.partial(conv_kernel, first, count),
        out_shape=jax.ShapeDtypeStruct((ROWS, count * 1024 + extra), BF),
        in_specs=[pl.BlockSpec(memory_space=pltpu.SMEM)] + [pl.BlockSpec(memory_space=pltpu.VMEM)] * 6
        + [pl.BlockSpec(memory_space=pl.ANY)] * len(after),
        out_specs=pl.BlockSpec(memory_space=pltpu.VMEM),
        scratch_shapes=[pltpu.VMEM((256, 1024), BF)],
        compiler_params=pltpu.CompilerParams(vmem_limit_bytes=40 * 2**20),
        cost_estimate=pl.CostEstimate(flops=count * 2 * 86400 * 256 * 256, bytes_accessed=8 * 2**20, transcendentals=0),
        name="conv",
    )(nblk, win, half, w, sel, bias, lab, *after)


TILES = 16
OWNED = 20
SLOTS = 25
NOTE = 4
FIRST = 5
NTILES = 136
GROUP = 1536
CLASSES = 1000
FEAT = 8


COMMON = tuple((96 * k, 96) for k in range(8)) + ((768, 384),)
BLOCKS = (COMMON + ((1152, 288), (1440, 96)), COMMON + tuple((1152 + 96 * k, 96) for k in range(4)))
COUNT = len(BLOCKS[0]) + len(BLOCKS[1])


def gram_kernel(me_ref, owner_ref, *refs):
    n = len(BLOCKS[0])
    parts, (out_ref, peak_ref) = (refs[:n], refs[n:COUNT]), refs[COUNT:COUNT + 2]
    fa_ref, fb_ref, ft_ref, target_ref, left_ref, list_i, list_j, sem = refs[COUNT + 2:]
    held = (fa_ref, fb_ref)
    me_tile = me_ref[0]
    copies = [
        [
            pltpu.make_async_copy(ref, held[part].at[start:start + size], sem.at[part * n + k])
            for k, (ref, (start, size)) in enumerate(zip(parts[part], BLOCKS[part]))
        ]
        for part in range(2)
    ]
    for group in copies:
        for copy in group:
            copy.start()

    def scan(k, carry):
        i, j, n = carry
        mine = owner_ref[k] == me_tile

        @pl.when(mine)
        def _():
            list_i[n] = i
            list_j[n] = j

        wrap = j == TILES - 1
        i2 = jnp.where(wrap, i + 1, i)
        return i2, jnp.where(wrap, i2, j + 1), n + mine.astype(jnp.int32)

    _, _, owned = lax.fori_loop(0, NTILES, scan, (jnp.int32(0), jnp.int32(0), jnp.int32(0)))
    peak_ref[...] = jnp.zeros_like(peak_ref)

    @pl.loop(owned, OWNED)
    def _(slot):
        for k in range(FEAT):
            out_ref[k, slot + FIRST] = jnp.zeros((32, 256), F32)

    for part in range(2):
        for copy in copies[part]:
            copy.wait()
        for local in range(2):
            for q in range(4):
                cols = slice(local * 1024 + q * 256, local * 1024 + (q + 1) * 256)
                ft_ref[q * 4 + part * 2 + local] = held[part][:, cols].T
    digit = lax.broadcasted_iota(jnp.int32, (128, 256), 0)
    weight = jnp.where(digit == 0, 8.0, jnp.where(digit == 1, 1.0, 0.0)).astype(BF)
    label = dot(fa_ref[:, 2048:], weight)
    classes = lax.broadcasted_iota(jnp.int32, (GROUP, 256), 1).astype(F32)
    for s in range(4):
        target_ref[:, s * 256:(s + 1) * 256] = jnp.where(label == classes + 256.0 * s, 1.0, -1.0).astype(BF)

    def put(slot, product):
        peak_ref[...] = jnp.maximum(peak_ref[...], jnp.max(jnp.abs(product).reshape(32, 8, 256), axis=0))
        for k in range(FEAT):
            out_ref[k, slot] = product[k * 32:(k + 1) * 32, :]

    start = pl.multiple_of(me_tile % 8 * 32, 32)
    for f in range(FEAT):
        t = f // 2 * 4 + f % 2 * 2 + me_tile // 8
        left_ref[f * 32:(f + 1) * 32, :] = ft_ref[t, pl.ds(start, 32), :]
    for s in range(4):
        put(s, dot(left_ref[...], target_ref[:, s * 256:(s + 1) * 256]))
    for s in range(0, FEAT, 2):
        out_ref[s:s + 2, NOTE] = jnp.zeros((2, 32, 256), F32)

    @pl.loop(0, owned)
    def _(slot):
        j = list_j[slot]
        at = pl.multiple_of(j % 2 * 1024 + j // 4 * 256, 256)
        second = j % 4 >= 2

        @pl.when(second)
        def _():
            put(slot + FIRST, dot(ft_ref[list_i[slot]], fb_ref[:, pl.ds(at, 256)]))

        @pl.when(jnp.logical_not(second))
        def _():
            put(slot + FIRST, dot(ft_ref[list_i[slot]], fa_ref[:, pl.ds(at, 256)]))


def gram(me, tile_owner, parts):
    smem = pl.BlockSpec(memory_space=pltpu.SMEM)
    vmem = pl.BlockSpec(memory_space=pltpu.VMEM)
    return pl.pallas_call(
        gram_kernel,
        out_shape=(jax.ShapeDtypeStruct((FEAT, SLOTS, 32, 256), F32), jax.ShapeDtypeStruct((8, 256), F32)),
        in_specs=[smem, smem] + [pl.BlockSpec(memory_space=pltpu.HBM)] * COUNT,
        out_specs=(vmem, vmem),
        scratch_shapes=[
            pltpu.VMEM((GROUP, 2176), BF),
            pltpu.VMEM((GROUP, 2048), BF),
            pltpu.VMEM((TILES, 256, GROUP), BF),
            pltpu.VMEM((GROUP, 1024), BF),
            pltpu.VMEM((256, GROUP), BF),
            pltpu.SMEM((OWNED,), jnp.int32),
            pltpu.SMEM((OWNED,), jnp.int32),
            pltpu.SemaphoreType.DMA((COUNT,)),
        ],
        compiler_params=pltpu.CompilerParams(vmem_limit_bytes=56 * 2**20),
        cost_estimate=pl.CostEstimate(flops=5 * 10**9, bytes_accessed=20 * 2**20, transcendentals=0),
        name="gram",
    )(me, tile_owner, *parts[0], *parts[1])


HALF = jnp.float16


STEPS = (8, 12, 20)


def exchange(partial, peak, owned):
    exponent = jnp.floor(jnp.log2(jnp.maximum(jnp.max(peak), 1e-30)))
    scale = jnp.exp2(13.0 - exponent)

    def some(count, partial):
        used = partial[:, :FIRST + count]
        note = lax.broadcasted_iota(jnp.int32, used.shape, 1) == NOTE
        coded = jnp.where(note, exponent, used * scale).astype(HALF)
        got = lax.all_to_all(coded, "feat", split_axis=0, concat_axis=0, tiled=True)
        back = jnp.exp2(got[:, NOTE:FIRST, :1, :1].astype(F32) - 13.0) * (1.0 / 12288.0)
        total = jnp.sum(got.astype(F32) * back, axis=0)
        cross = total[:NOTE].transpose(1, 0, 2).reshape(32, 1024)[:, :CLASSES]
        return jnp.pad(total[FIRST:], ((0, OWNED - count), (0, 0), (0, 0))), cross

    level = sum((owned > step).astype(jnp.int32) for step in STEPS[:-1])
    return lax.switch(level, [functools.partial(some, step) for step in STEPS], partial)


def hop(dy=0, dx=0, core=0):
    def index(y, x, c):
        return (y % 2 * 4 + x % 4) * 2 + c % 2

    return [(index(y, x, c), index(y + dy, x + dx, c + core)) for y in range(2) for x in range(4) for c in range(2)]


def onward():
    return [(s, d) if s % 2 == 0 else (s, e) for (s, d), (_, e) in zip(hop(dx=1), hop(dx=-1))]


def send(block, perm):
    return lax.ppermute(block, "tile", perm)


def spread_first(own):
    left = send(own, hop(dx=1))
    right = send(own, hop(dx=-1))
    over = send(own, hop(dy=1))
    return own, over, left, right


def spread_second(first, earlier=None):
    own, over, left, right = first
    even = lax.axis_index("tile") % 2 == 0
    far = send(jnp.where(even, left, right), onward())
    if earlier is not None:
        over, far, *earlier[7:10] = lax.optimization_barrier((over, far, *earlier[7:10]))
    over_left = send(over, hop(dx=1))
    over_right = send(over, hop(dx=-1))
    swap_a = send(jnp.concatenate([own, over, left, right], axis=0), hop(core=1))
    return far, over_left, over_right, swap_a


def spread_third(first, second, apart):
    own, over, left, right = first
    far, over_left, over_right, swap_a = second
    even = lax.axis_index("tile") % 2 == 0
    over_far = send(far, hop(dy=1)) if apart else send(jnp.where(even, over_left, over_right), onward())
    held = [own, over, left, right, over_left, over_right, far, over_far, swap_a]
    if apart:
        far_swap = send(far, hop(core=1))
        rest = lax.optimization_barrier((over_left, over_right, over_far))
        swaps = [send(block, hop(core=1)) for block in rest]
        return held + [swaps[0], swaps[1], far_swap, swaps[2]]
    swap_b = send(jnp.concatenate([over_left, over_right, far], axis=0), hop(core=1))
    return held + [swap_b, send(over_far, hop(core=1))]


def body(images, row_list, labels, filters, bias, tile_owner):
    win, half, w, sel, lab, nblk = prep(images, row_list, labels, filters)
    bias4 = bias.reshape(4, 1, 256)
    own_a = conv(0, 2, nblk, win, half, w, sel, bias4, lab, 128)
    first_a = spread_first(own_a)
    own_b2 = conv(2, 1, nblk, win, half, w, sel, bias4, lab, 0, (own_a,))
    second_a = spread_second(first_a)
    own_b3 = conv(3, 1, nblk, win, half, w, sel, bias4, lab, 0, first_a[1:])
    own_b = jnp.concatenate([own_b2, own_b3], axis=1)
    own_b, far, over_left, over_right = lax.optimization_barrier((own_b,) + second_a[:3])
    second_a = (far, over_left, over_right, second_a[3])
    first_b = spread_first(own_b)
    part_a = spread_third(first_a, second_a, False)
    second_b = spread_second(first_b, part_a)
    part_b = spread_third(first_b, second_b, True)
    me = jnp.stack([lax.axis_index("tile"), lax.axis_index("feat")]).astype(jnp.int32)
    partial, peak = gram(me, tile_owner, (part_a, part_b))
    owned = jnp.sum((tile_owner == me[0]).astype(jnp.int32))
    return exchange(partial, peak, owned)


def solution(mesh):
    def run(*args):
        return jax.shard_map(
            body,
            mesh=mesh,
            in_specs=(P(("feat", "tile"), None), P(("feat", "tile")), P(("feat", "tile")), P(), P(), P()),
            out_specs=(P("tile", "feat", None), P(("feat", "tile"), None)),
            check_vma=False,
        )(*args)

    return run
```

```python
import functools

import jax
import jax.numpy as jnp
from jax import lax
from jax.experimental import pallas as pl
from jax.experimental.pallas import tpu as pltpu
from jax.sharding import PartitionSpec as P

ROWS = 96
BLK = 16
NBLK = 6
WIDE = 112
BF = jnp.bfloat16
F32 = jnp.float32
LAG = 3


def dot(a, b, dims=(((1,), (0,)), ((), ()))):
    return lax.dot_general(a, b, dims, preferred_element_type=F32)


def prep_kernel(me_ref, owner_ref, rows_ref, labels_ref, filt_ref, img_hbm, win_ref, half_ref, w_ref, sel_ref, lab_ref, nblk_ref, img_ref, x_ref, pick_ref, flat_ref, sem):
    fetch = pltpu.make_async_copy(img_hbm, img_ref, sem)
    fetch.start()
    flat_ref[...] = jnp.zeros_like(flat_ref)
    for i in range(6):
        for j in range(6):
            p = 6 * i + j
            flat_ref[3 * p:3 * p + 3, :] = filt_ref[i, j].astype(F32)
    rows_i = lax.broadcasted_iota(jnp.int32, (1536, 128), 0)
    cols_i = lax.broadcasted_iota(jnp.int32, (1536, 128), 1)
    d = rows_i // 256
    di = d // 3
    dj = d - 3 * di
    r = rows_i % 256 // 32 - 2 * di
    c = rows_i % 32 - 6 * dj
    ok = (r >= 0) & (r < 6) & (c >= 0) & (c < 18)
    spread = jnp.where(ok & (cols_i == r * 18 + c), 1.0, 0.0).astype(BF)
    for nc in range(4):
        w_ref[nc] = dot(spread, flat_ref[:, nc * 256:(nc + 1) * 256].astype(BF)).astype(BF)

    lanes = lax.broadcasted_iota(jnp.int32, (ROWS, 128), 1)
    subs = lax.broadcasted_iota(jnp.int32, (ROWS, 128), 0)
    rows = jnp.broadcast_to(rows_ref[...], (128, 128)).astype(F32).T[:ROWS]
    hit = rows.astype(jnp.int32) == lanes
    used = jnp.max(jnp.where(hit, 1.0, 0.0), axis=0, keepdims=True)
    low = lax.broadcasted_iota(jnp.int32, (128, 128), 0)
    high = lax.broadcasted_iota(jnp.int32, (128, 128), 1)
    upto = jnp.where(low <= high, 1.0, 0.0).astype(BF)
    rank = dot(jnp.broadcast_to(used, (16, 128)).astype(BF), upto)[0:1] - 1.0
    rank = rank.astype(jnp.int32)
    total = jnp.sum(used).astype(jnp.int32)
    whole = (total + 7) // BLK
    nblk_ref[0, 0] = whole
    nblk_ref[0, 1] = total - whole * BLK
    nblk_ref[0, 2] = me_ref[0]
    nblk_ref[0, 3] = jnp.sum(jnp.where(owner_ref[...] == me_ref[0], 1.0, 0.0)).astype(jnp.int32)
    deep = lax.broadcasted_iota(jnp.int32, (WIDE, 128), 0)
    deep = jnp.where(deep < ROWS, deep, jnp.where(deep < ROWS + 8, deep - ROWS + BLK * whole, -1))
    take = jnp.where((deep == rank) & (used > 0.0), 1.0, 0.0).astype(BF)
    compact = take[:ROWS]
    sel_ref[:, :ROWS] = dot(jnp.where(hit, 1.0, 0.0).astype(BF), compact, (((1,), (1,)), ((), ()))).astype(BF)
    sel_ref[:, ROWS:] = jnp.zeros((ROWS, 256 - ROWS), BF)
    label = jnp.sum(jnp.where(hit, labels_ref[...], 0), axis=1, keepdims=True)
    coarse = label // 8
    fine = label - coarse * 8
    lab_ref[...] = jnp.where(lanes == 0, coarse, jnp.where(lanes == 1, fine, 0)).astype(BF)
    col = lax.broadcasted_iota(jnp.int32, (1, 1280), 1)
    within = col % 32
    source = (col % 128) // 32 * 192 + 18 * (col // 128) + within
    source = jnp.where(within < 30, source, -1)
    place = lax.broadcasted_iota(jnp.int32, (768, 1280), 0)
    pick_ref[...] = jnp.where(place == source, 1.0, 0.0).astype(BF)
    fetch.wait()
    for part in range(16):
        x_ref[part * WIDE:(part + 1) * WIDE, :] = dot(take[:, :ROWS], img_ref[:, part * 768:(part + 1) * 768]).astype(BF)

    @pl.loop(0, 5)
    def _(n):
        fine = dot(x_ref[...], pick_ref[:, pl.ds(pl.multiple_of(n * 256, 256), 256)])
        tile = fine.astype(BF)
        for part in range(16):
            row = part * WIDE + ROWS
            pair = jnp.concatenate([fine[row:row + 8, :128], fine[row:row + 8, 128:]], axis=0)
            half_ref[part, pl.ds(pl.multiple_of(n * 16, 16), 16), :] = pair.astype(BF)
        for h in range(2):
            at = pl.multiple_of((2 * n + h) * 16, 16)
            for part in range(16):
                for b in range(NBLK):
                    row = part * WIDE + b * 16
                    win_ref[part, b, pl.ds(at, 16), :] = tile[row:row + 16, h * 128:(h + 1) * 128]


def prep(me, tile_owner, images, row_list, labels, filters):
    vmem = pl.BlockSpec(memory_space=pltpu.VMEM)
    return pl.pallas_call(
        prep_kernel,
        out_shape=(
            jax.ShapeDtypeStruct((16, NBLK, 160, 128), BF),
            jax.ShapeDtypeStruct((16, 80, 128), BF),
            jax.ShapeDtypeStruct((4, 1536, 256), BF),
            jax.ShapeDtypeStruct((ROWS, 256), BF),
            jax.ShapeDtypeStruct((ROWS, 128), BF),
            jax.ShapeDtypeStruct((1, 4), jnp.int32),
        ),
        in_specs=[pl.BlockSpec(memory_space=pltpu.SMEM), vmem, vmem, vmem, vmem, pl.BlockSpec(memory_space=pl.ANY)],
        out_specs=(vmem, vmem, vmem, vmem, vmem, pl.BlockSpec(memory_space=pltpu.SMEM)),
        scratch_shapes=[
            pltpu.VMEM((ROWS, 12288), BF),
            pltpu.VMEM((16 * WIDE, 768), BF),
            pltpu.VMEM((768, 1280), BF),
            pltpu.VMEM((128, 1024), F32),
            pltpu.SemaphoreType.DMA,
        ],
        compiler_params=pltpu.CompilerParams(vmem_limit_bytes=40 * 2**20),
        name="prep",
    )(me, jnp.pad(tile_owner, (0, 256 - NTILES), constant_values=-1).reshape(1, 256), jnp.pad(row_list, (0, 32)).reshape(1, 128), jnp.pad(labels, (0, 32)).reshape(1, 128), filters, images)


def conv_kernel(first, count, nblk_ref, win_ref, half_ref, w_ref, sel_ref, bias_ref, lab_ref, *refs):
    out_ref, uniq_ref = refs[-2:]
    uniq_ref[...] = jnp.zeros_like(uniq_ref)
    if out_ref.shape[1] > count * 1024:
        out_ref[:, count * 1024:] = lab_ref[...]
    steps = []
    for d in range(6):
        for w in range(15):
            steps.append((d, w, 0 if w <= (7 if d < 3 else 6) else 1))

    def block(nc, b, bias, floor, acc):
        total = [[jnp.zeros((16, 256), F32) for _ in range(2)] for _ in range(2)]

        def take(k):
            qr = steps[k][2]
            for m in range(2):
                got = pltpu.matmul_pop(acc[m][k % 8]).reshape(5, 16, 256)
                total[qr][m] = total[qr][m] + jnp.sum(jnp.maximum(got, floor[None]), axis=0)

        for k, (d, w, _) in enumerate(steps):
            if w == 0:
                for m in range(2):
                    pltpu.matmul_push_rhs(w_ref[first + nc, d * 256:(d + 1) * 256, :], d % 2, m)
            for m in range(2):
                rows = slice(m * 80, (m + 1) * 80)
                lhs = jnp.concatenate([win_ref[w, b, rows, :], win_ref[w + 1, b, rows, :]], axis=1)
                pltpu.matmul_acc_lhs(acc[m][k % 8], lhs, load_staged_rhs=d % 2 if w == 0 else None)
            if k >= LAG:
                take(k - LAG)
        for k in range(len(steps) - LAG, len(steps)):
            take(k)
        at = pl.multiple_of(b * 16, 16)
        for qr in range(2):
            for m in range(2):
                q = 2 * qr + m
                mean = (total[qr][m] + 225.0 * bias) * (1.0 / 225.0)
                uniq_ref[pl.ds(at, 16), q * 256:(q + 1) * 256] = mean.astype(BF)

    def half_block(nc, b, bias, floor, acc):
        total = [[jnp.zeros((8, 256), F32) for _ in range(2)] for _ in range(2)]
        low = floor[:8]

        def take(k):
            d, j = k // 8, k % 8
            for m in range(2):
                w = 2 * j + m
                if w < 15:
                    qr = 0 if w <= (7 if d < 3 else 6) else 1
                    got = jnp.maximum(pltpu.matmul_pop(acc[m][k % 8]).reshape(10, 8, 256), low[None])
                    total[qr][0] = total[qr][0] + jnp.sum(got[:5], axis=0)
                    total[qr][1] = total[qr][1] + jnp.sum(got[5:], axis=0)

        for k in range(48):
            d, j = k // 8, k % 8
            if j == 0:
                for m in range(2):
                    pltpu.matmul_push_rhs(w_ref[first + nc, d * 256:(d + 1) * 256, :], d % 2, m)
            for m in range(2):
                w = 2 * j + m
                if w < 15:
                    lhs = jnp.concatenate([half_ref[w], half_ref[w + 1]], axis=1)
                    pltpu.matmul_acc_lhs(acc[m][k % 8], lhs, load_staged_rhs=d % 2 if j == 0 else None)
            if k >= LAG:
                take(k - LAG)
        for k in range(48 - LAG, 48):
            take(k)
        at = pl.multiple_of(b * 16, 16)
        for q in range(4):
            mean = (total[q // 2][q % 2] + 225.0 * bias) * (1.0 / 225.0)
            uniq_ref[pl.ds(at, 16), q * 256:(q + 1) * 256] = jnp.concatenate([mean, jnp.zeros_like(mean)], axis=0).astype(BF)

    def scoped(*accs):
        @pl.loop(0, count)
        def _(nc):
            bias = bias_ref[first + nc]
            floor = jnp.broadcast_to(-bias, (16, 256))

            @pl.loop(0, nblk_ref[0, 0])
            def _(b):
                block(nc, b, bias, floor, (accs[:8], accs[8:16]))

            @pl.when(nblk_ref[0, 1] > 0)
            def _():
                half_block(nc, nblk_ref[0, 0], bias, floor, (accs[:8], accs[8:16]))

            for m in range(2):
                for qr in range(2):
                    q = 2 * qr + m
                    pltpu.matmul_push_rhs(uniq_ref[:, q * 256:(q + 1) * 256], qr, m)
                    pltpu.matmul_acc_lhs(accs[16 + q], sel_ref[...], load_staged_rhs=qr)
            for q in range(4):
                at = pl.multiple_of(nc * 1024 + q * 256, 256)
                out_ref[:, pl.ds(at, 256)] = pltpu.matmul_pop(accs[16 + q]).astype(BF)

    pl.run_scoped(
        scoped,
        *[pltpu.ACC(m)((80, 256), F32) for m in range(2) for _ in range(8)],
        *[pltpu.ACC(q % 2)((ROWS, 256), F32) for q in range(4)],
    )


def conv(first, count, nblk, win, half, w, sel, bias, lab, extra, after=()):
    return pl.pallas_call(
        functools.partial(conv_kernel, first, count),
        out_shape=jax.ShapeDtypeStruct((ROWS, count * 1024 + extra), BF),
        in_specs=[pl.BlockSpec(memory_space=pltpu.SMEM)] + [pl.BlockSpec(memory_space=pltpu.VMEM)] * 6
        + [pl.BlockSpec(memory_space=pl.ANY)] * len(after),
        out_specs=pl.BlockSpec(memory_space=pltpu.VMEM),
        scratch_shapes=[pltpu.VMEM((256, 1024), BF)],
        compiler_params=pltpu.CompilerParams(vmem_limit_bytes=40 * 2**20),
        cost_estimate=pl.CostEstimate(flops=count * 2 * 86400 * 256 * 256, bytes_accessed=8 * 2**20, transcendentals=0),
        name="conv",
    )(nblk, win, half, w, sel, bias, lab, *after)


TILES = 16
OWNED = 20
SLOTS = 25
NOTE = 4
FIRST = 5
NTILES = 136
GROUP = 1536
CLASSES = 1000
FEAT = 8


BLOCKS = ((0, 96), (96, 96), (192, 96), (288, 96), (384, 96), (480, 96), (576, 96), (672, 96), (768, 384), (1152, 288), (1440, 96))


def gram_kernel(me_ref, owner_ref, *refs):
    n = len(BLOCKS)
    parts, (out_ref, peak_ref) = (refs[:n], refs[n:2 * n]), refs[2 * n:2 * n + 2]
    fa_ref, fb_ref, ft_ref, target_ref, left_ref, list_i, list_j, sem = refs[2 * n + 2:]
    held = (fa_ref, fb_ref)
    me_tile = me_ref[0, 2]
    copies = [
        [
            pltpu.make_async_copy(ref, held[part].at[start:start + size], sem.at[part * n + k])
            for k, (ref, (start, size)) in enumerate(zip(parts[part], BLOCKS))
        ]
        for part in range(2)
    ]
    for group in copies:
        for copy in group:
            copy.start()

    def scan(k, carry):
        i, j, n = carry
        mine = owner_ref[k] == me_tile

        @pl.when(mine)
        def _():
            list_i[n] = i
            list_j[n] = j

        wrap = j == TILES - 1
        i2 = jnp.where(wrap, i + 1, i)
        return i2, jnp.where(wrap, i2, j + 1), n + mine.astype(jnp.int32)

    _, _, owned = lax.fori_loop(0, NTILES, scan, (jnp.int32(0), jnp.int32(0), jnp.int32(0)))
    peak_ref[...] = jnp.zeros_like(peak_ref)

    @pl.loop(owned, OWNED)
    def _(slot):
        for k in range(FEAT):
            out_ref[k, slot + FIRST] = jnp.zeros((32, 256), F32)

    for part in range(2):
        for copy in copies[part]:
            copy.wait()
        for local in range(2):
            for q in range(4):
                cols = slice(local * 1024 + q * 256, local * 1024 + (q + 1) * 256)
                ft_ref[q * 4 + part * 2 + local] = held[part][:, cols].T
    digit = lax.broadcasted_iota(jnp.int32, (128, 256), 0)
    weight = jnp.where(digit == 0, 8.0, jnp.where(digit == 1, 1.0, 0.0)).astype(BF)
    label = dot(fa_ref[:, 2048:], weight)
    classes = lax.broadcasted_iota(jnp.int32, (GROUP, 256), 1).astype(F32)
    for s in range(4):
        target_ref[:, s * 256:(s + 1) * 256] = jnp.where(label == classes + 256.0 * s, 1.0, -1.0).astype(BF)

    def put(slot, product):
        peak_ref[...] = jnp.maximum(peak_ref[...], jnp.max(jnp.abs(product).reshape(32, 8, 256), axis=0))
        for k in range(FEAT):
            out_ref[k, slot] = product[k * 32:(k + 1) * 32, :]

    start = pl.multiple_of(me_tile % 8 * 32, 32)
    for f in range(FEAT):
        t = f // 2 * 4 + f % 2 * 2 + me_tile // 8
        left_ref[f * 32:(f + 1) * 32, :] = ft_ref[t, pl.ds(start, 32), :]
    for s in range(4):
        put(s, dot(left_ref[...], target_ref[:, s * 256:(s + 1) * 256]))
    for s in range(0, FEAT, 2):
        out_ref[s:s + 2, NOTE] = jnp.zeros((2, 32, 256), F32)

    @pl.loop(0, owned)
    def _(slot):
        j = list_j[slot]
        at = pl.multiple_of(j % 2 * 1024 + j // 4 * 256, 256)
        second = j % 4 >= 2

        @pl.when(second)
        def _():
            put(slot + FIRST, dot(ft_ref[list_i[slot]], fb_ref[:, pl.ds(at, 256)]))

        @pl.when(jnp.logical_not(second))
        def _():
            put(slot + FIRST, dot(ft_ref[list_i[slot]], fa_ref[:, pl.ds(at, 256)]))

    top = jnp.max(jnp.max(peak_ref[...], axis=1, keepdims=True), axis=0, keepdims=True)
    exponent = jnp.floor(jnp.log2(jnp.maximum(jnp.broadcast_to(top, (8, 256)), 1e-30)))
    row = lax.broadcasted_iota(jnp.int32, (8, 256), 0)
    peak_ref[...] = jnp.where(row == 0, exponent, jnp.exp2(13.0 - exponent))


def gram(me, tile_owner, parts):
    smem = pl.BlockSpec(memory_space=pltpu.SMEM)
    vmem = pl.BlockSpec(memory_space=pltpu.VMEM)
    return pl.pallas_call(
        gram_kernel,
        out_shape=(jax.ShapeDtypeStruct((FEAT, SLOTS, 32, 256), F32), jax.ShapeDtypeStruct((8, 256), F32)),
        in_specs=[smem, smem] + [pl.BlockSpec(memory_space=pltpu.HBM)] * (2 * len(BLOCKS)),
        out_specs=(vmem, vmem),
        scratch_shapes=[
            pltpu.VMEM((GROUP, 2176), BF),
            pltpu.VMEM((GROUP, 2048), BF),
            pltpu.VMEM((TILES, 256, GROUP), BF),
            pltpu.VMEM((GROUP, 1024), BF),
            pltpu.VMEM((256, GROUP), BF),
            pltpu.SMEM((OWNED,), jnp.int32),
            pltpu.SMEM((OWNED,), jnp.int32),
            pltpu.SemaphoreType.DMA((2 * len(BLOCKS),)),
        ],
        compiler_params=pltpu.CompilerParams(vmem_limit_bytes=56 * 2**20),
        cost_estimate=pl.CostEstimate(flops=5 * 10**9, bytes_accessed=20 * 2**20, transcendentals=0),
        name="gram",
    )(me, tile_owner, *parts[0], *parts[1])


HALF = jnp.float16


STEPS = (8, 12, 20)


def exchange(partial, peak, owned):
    exponent = peak[0].reshape(1, 1, 1, 256)
    scale = peak[1].reshape(1, 1, 1, 256)

    def some(count, partial):
        used = partial[:, :FIRST + count]
        note = lax.broadcasted_iota(jnp.int32, used.shape, 1) == NOTE
        coded = jnp.where(note, exponent, used * scale).astype(HALF)
        got = lax.all_to_all(coded, "feat", split_axis=0, concat_axis=0, tiled=True)
        back = jnp.exp2(got[:, NOTE:FIRST, :1, :1].astype(F32) - 13.0) * (1.0 / 12288.0)
        total = jnp.sum(got.astype(F32) * back, axis=0)
        cross = total[:NOTE].transpose(1, 0, 2).reshape(32, 1024)[:, :CLASSES]
        return jnp.pad(total[FIRST:], ((0, OWNED - count), (0, 0), (0, 0))), cross

    level = sum((owned > step).astype(jnp.int32) for step in STEPS[:-1])
    return lax.switch(level, [functools.partial(some, step) for step in STEPS], partial)


def hop(dy=0, dx=0, core=0):
    def index(y, x, c):
        return (y % 2 * 4 + x % 4) * 2 + c % 2

    return [(index(y, x, c), index(y + dy, x + dx, c + core)) for y in range(2) for x in range(4) for c in range(2)]


def onward():
    return [(s, d) if s % 2 == 0 else (s, e) for (s, d), (_, e) in zip(hop(dx=1), hop(dx=-1))]


def send(block, perm):
    return lax.ppermute(block, "tile", perm)


def spread_first(own):
    left = send(own, hop(dx=1))
    right = send(own, hop(dx=-1))
    over = send(own, hop(dy=1))
    return own, over, left, right


def spread_second(first):
    own, over, left, right = first
    even = lax.axis_index("tile") % 2 == 0
    far = send(jnp.where(even, left, right), onward())
    over_left = send(over, hop(dx=1))
    over_right = send(over, hop(dx=-1))
    swap_a = send(jnp.concatenate([own, over, left, right], axis=0), hop(core=1))
    return far, over_left, over_right, swap_a


def spread_third(first, second):
    own, over, left, right = first
    far, over_left, over_right, swap_a = second
    even = lax.axis_index("tile") % 2 == 0
    over_far = send(jnp.where(even, over_left, over_right), onward())
    swap_b = send(jnp.concatenate([over_left, over_right, far], axis=0), hop(core=1))
    swap_c = send(over_far, hop(core=1))
    return [own, over, left, right, over_left, over_right, far, over_far, swap_a, swap_b, swap_c]


def body(images, row_list, labels, filters, bias, tile_owner):
    me = lax.axis_index("tile").astype(jnp.int32).reshape(1)
    win, half, w, sel, lab, nblk = prep(me, tile_owner, images, row_list, labels, filters)
    bias4 = bias.reshape(4, 1, 256)
    own_a = conv(0, 2, nblk, win, half, w, sel, bias4, lab, 128)
    first_a = spread_first(own_a)
    own_b2 = conv(2, 1, nblk, win, half, w, sel, bias4, lab, 0, (own_a,))
    second_a = spread_second(first_a)
    own_b3 = conv(3, 1, nblk, win, half, w, sel, bias4, lab, 0, first_a[1:])
    own_b = jnp.concatenate([own_b2, own_b3], axis=1)
    own_b, far, over_left, over_right = lax.optimization_barrier((own_b,) + second_a[:3])
    second_a = (far, over_left, over_right, second_a[3])
    first_b = spread_first(own_b)
    part_a = spread_third(first_a, second_a)
    second_b = spread_second(first_b)
    part_b = spread_third(first_b, second_b)
    partial, peak = gram(nblk, tile_owner, (part_a, part_b))
    return exchange(partial, peak, nblk[0, 3])


def solution(mesh):
    def run(*args):
        return jax.shard_map(
            body,
            mesh=mesh,
            in_specs=(P(("feat", "tile"), None), P(("feat", "tile")), P(("feat", "tile")), P(), P(), P()),
            out_specs=(P("tile", "feat", None), P(("feat", "tile"), None)),
            check_vma=False,
        )(*args)

    return run
```

```python
import functools

import jax
import jax.numpy as jnp
from jax import lax
from jax.experimental import pallas as pl
from jax.experimental.pallas import tpu as pltpu
from jax.sharding import PartitionSpec as P

ROWS = 96
BLK = 16
NBLK = 6
WIDE = 112
BF = jnp.bfloat16
F32 = jnp.float32
LAG = 3


def dot(a, b, dims=(((1,), (0,)), ((), ()))):
    return lax.dot_general(a, b, dims, preferred_element_type=F32)


def prep_kernel(me_ref, owner_ref, rows_ref, labels_ref, filt_ref, img_hbm, win_ref, half_ref, w_ref, sel_ref, lab_ref, nblk_ref, img_ref, x_ref, pick_ref, flat_ref, sem):
    fetch = pltpu.make_async_copy(img_hbm, img_ref, sem)
    fetch.start()
    flat_ref[...] = jnp.zeros_like(flat_ref)
    for i in range(6):
        for j in range(6):
            p = 6 * i + j
            flat_ref[3 * p:3 * p + 3, :] = filt_ref[i, j].astype(F32)
    rows_i = lax.broadcasted_iota(jnp.int32, (1536, 128), 0)
    cols_i = lax.broadcasted_iota(jnp.int32, (1536, 128), 1)
    d = rows_i // 256
    di = d // 3
    dj = d - 3 * di
    r = rows_i % 256 // 32 - 2 * di
    c = rows_i % 32 - 6 * dj
    ok = (r >= 0) & (r < 6) & (c >= 0) & (c < 18)
    spread = jnp.where(ok & (cols_i == r * 18 + c), 1.0, 0.0).astype(BF)
    for nc in range(4):
        w_ref[nc] = dot(spread, flat_ref[:, nc * 256:(nc + 1) * 256].astype(BF)).astype(BF)

    lanes = lax.broadcasted_iota(jnp.int32, (ROWS, 128), 1)
    subs = lax.broadcasted_iota(jnp.int32, (ROWS, 128), 0)
    rows = jnp.broadcast_to(rows_ref[...], (128, 128)).astype(F32).T[:ROWS]
    hit = rows.astype(jnp.int32) == lanes
    used = jnp.max(jnp.where(hit, 1.0, 0.0), axis=0, keepdims=True)
    low = lax.broadcasted_iota(jnp.int32, (128, 128), 0)
    high = lax.broadcasted_iota(jnp.int32, (128, 128), 1)
    upto = jnp.where(low <= high, 1.0, 0.0).astype(BF)
    rank = dot(jnp.broadcast_to(used, (16, 128)).astype(BF), upto)[0:1] - 1.0
    rank = rank.astype(jnp.int32)
    total = jnp.sum(used).astype(jnp.int32)
    whole = (total + 7) // BLK
    nblk_ref[0, 0] = whole
    nblk_ref[0, 1] = total - whole * BLK
    nblk_ref[0, 2] = me_ref[0]
    nblk_ref[0, 3] = jnp.sum(jnp.where(owner_ref[...] == me_ref[0], 1.0, 0.0)).astype(jnp.int32)
    deep = lax.broadcasted_iota(jnp.int32, (WIDE, 128), 0)
    deep = jnp.where(deep < ROWS, deep, jnp.where(deep < ROWS + 8, deep - ROWS + BLK * whole, -1))
    take = jnp.where((deep == rank) & (used > 0.0), 1.0, 0.0).astype(BF)
    compact = take[:ROWS]
    sel_ref[:, :ROWS] = dot(jnp.where(hit, 1.0, 0.0).astype(BF), compact, (((1,), (1,)), ((), ()))).astype(BF)
    sel_ref[:, ROWS:] = jnp.zeros((ROWS, 256 - ROWS), BF)
    label = jnp.sum(jnp.where(hit, labels_ref[...], 0), axis=1, keepdims=True)
    coarse = label // 8
    fine = label - coarse * 8
    lab_ref[...] = jnp.where(lanes == 0, coarse, jnp.where(lanes == 1, fine, 0)).astype(BF)
    col = lax.broadcasted_iota(jnp.int32, (1, 1280), 1)
    within = col % 32
    source = (col % 128) // 32 * 192 + 18 * (col // 128) + within
    source = jnp.where(within < 30, source, -1)
    place = lax.broadcasted_iota(jnp.int32, (768, 1280), 0)
    pick_ref[...] = jnp.where(place == source, 1.0, 0.0).astype(BF)
    fetch.wait()
    for part in range(16):
        x_ref[part * WIDE:(part + 1) * WIDE, :] = dot(take[:, :ROWS], img_ref[:, part * 768:(part + 1) * 768]).astype(BF)

    @pl.loop(0, 5)
    def _(n):
        fine = dot(x_ref[...], pick_ref[:, pl.ds(pl.multiple_of(n * 256, 256), 256)])
        tile = fine.astype(BF)
        for part in range(16):
            row = part * WIDE + ROWS
            pair = jnp.concatenate([fine[row:row + 8, :128], fine[row:row + 8, 128:]], axis=0)
            half_ref[part, pl.ds(pl.multiple_of(n * 16, 16), 16), :] = pair.astype(BF)
        for h in range(2):
            at = pl.multiple_of((2 * n + h) * 16, 16)
            for part in range(16):
                for b in range(NBLK):
                    row = part * WIDE + b * 16
                    win_ref[part, b, pl.ds(at, 16), :] = tile[row:row + 16, h * 128:(h + 1) * 128]


def prep(me, tile_owner, images, row_list, labels, filters):
    vmem = pl.BlockSpec(memory_space=pltpu.VMEM)
    return pl.pallas_call(
        prep_kernel,
        out_shape=(
            jax.ShapeDtypeStruct((16, NBLK, 160, 128), BF),
            jax.ShapeDtypeStruct((16, 80, 128), BF),
            jax.ShapeDtypeStruct((4, 1536, 256), BF),
            jax.ShapeDtypeStruct((ROWS, 256), BF),
            jax.ShapeDtypeStruct((ROWS, 128), BF),
            jax.ShapeDtypeStruct((1, 4), jnp.int32),
        ),
        in_specs=[pl.BlockSpec(memory_space=pltpu.SMEM), vmem, vmem, vmem, vmem, pl.BlockSpec(memory_space=pl.ANY)],
        out_specs=(vmem, vmem, vmem, vmem, vmem, pl.BlockSpec(memory_space=pltpu.SMEM)),
        scratch_shapes=[
            pltpu.VMEM((ROWS, 12288), BF),
            pltpu.VMEM((16 * WIDE, 768), BF),
            pltpu.VMEM((768, 1280), BF),
            pltpu.VMEM((128, 1024), F32),
            pltpu.SemaphoreType.DMA,
        ],
        compiler_params=pltpu.CompilerParams(vmem_limit_bytes=40 * 2**20),
        name="prep",
    )(me, tile_owner.reshape(1, NTILES), jnp.pad(row_list, (0, 32)).reshape(1, 128), jnp.pad(labels, (0, 32)).reshape(1, 128), filters, images)


def conv_kernel(first, count, nblk_ref, win_ref, half_ref, w_ref, sel_ref, bias_ref, lab_ref, *refs):
    out_ref, uniq_ref = refs[-2:]
    uniq_ref[...] = jnp.zeros_like(uniq_ref)
    if out_ref.shape[1] > count * 1024:
        out_ref[:, count * 1024:] = lab_ref[...]
    steps = []
    for d in range(6):
        for w in range(15):
            steps.append((d, w, 0 if w <= (7 if d < 3 else 6) else 1))

    def block(nc, b, bias, floor, acc):
        total = [[jnp.zeros((16, 256), F32) for _ in range(2)] for _ in range(2)]

        def take(k):
            qr = steps[k][2]
            for m in range(2):
                got = pltpu.matmul_pop(acc[m][k % 8]).reshape(5, 16, 256)
                total[qr][m] = total[qr][m] + jnp.sum(jnp.maximum(got, floor[None]), axis=0)

        for k, (d, w, _) in enumerate(steps):
            if w == 0:
                for m in range(2):
                    pltpu.matmul_push_rhs(w_ref[first + nc, d * 256:(d + 1) * 256, :], d % 2, m)
            for m in range(2):
                rows = slice(m * 80, (m + 1) * 80)
                lhs = jnp.concatenate([win_ref[w, b, rows, :], win_ref[w + 1, b, rows, :]], axis=1)
                pltpu.matmul_acc_lhs(acc[m][k % 8], lhs, load_staged_rhs=d % 2 if w == 0 else None)
            if k >= LAG:
                take(k - LAG)
        for k in range(len(steps) - LAG, len(steps)):
            take(k)
        at = pl.multiple_of(b * 16, 16)
        for qr in range(2):
            for m in range(2):
                q = 2 * qr + m
                mean = (total[qr][m] + 225.0 * bias) * (1.0 / 225.0)
                uniq_ref[pl.ds(at, 16), q * 256:(q + 1) * 256] = mean.astype(BF)

    def half_block(nc, b, bias, floor, acc):
        total = [[jnp.zeros((8, 256), F32) for _ in range(2)] for _ in range(2)]
        low = floor[:8]

        def take(k):
            d, j = k // 8, k % 8
            for m in range(2):
                w = 2 * j + m
                if w < 15:
                    qr = 0 if w <= (7 if d < 3 else 6) else 1
                    got = jnp.maximum(pltpu.matmul_pop(acc[m][k % 8]).reshape(10, 8, 256), low[None])
                    total[qr][0] = total[qr][0] + jnp.sum(got[:5], axis=0)
                    total[qr][1] = total[qr][1] + jnp.sum(got[5:], axis=0)

        for k in range(48):
            d, j = k // 8, k % 8
            if j == 0:
                for m in range(2):
                    pltpu.matmul_push_rhs(w_ref[first + nc, d * 256:(d + 1) * 256, :], d % 2, m)
            for m in range(2):
                w = 2 * j + m
                if w < 15:
                    lhs = jnp.concatenate([half_ref[w], half_ref[w + 1]], axis=1)
                    pltpu.matmul_acc_lhs(acc[m][k % 8], lhs, load_staged_rhs=d % 2 if j == 0 else None)
            if k >= LAG:
                take(k - LAG)
        for k in range(48 - LAG, 48):
            take(k)
        at = pl.multiple_of(b * 16, 16)
        for q in range(4):
            mean = (total[q // 2][q % 2] + 225.0 * bias) * (1.0 / 225.0)
            uniq_ref[pl.ds(at, 16), q * 256:(q + 1) * 256] = jnp.concatenate([mean, jnp.zeros_like(mean)], axis=0).astype(BF)

    def scoped(*accs):
        @pl.loop(0, count)
        def _(nc):
            bias = bias_ref[first + nc]
            floor = jnp.broadcast_to(-bias, (16, 256))

            @pl.loop(0, nblk_ref[0, 0])
            def _(b):
                block(nc, b, bias, floor, (accs[:8], accs[8:16]))

            @pl.when(nblk_ref[0, 1] > 0)
            def _():
                half_block(nc, nblk_ref[0, 0], bias, floor, (accs[:8], accs[8:16]))

            for m in range(2):
                for qr in range(2):
                    q = 2 * qr + m
                    pltpu.matmul_push_rhs(uniq_ref[:, q * 256:(q + 1) * 256], qr, m)
                    pltpu.matmul_acc_lhs(accs[16 + q], sel_ref[...], load_staged_rhs=qr)
            for q in range(4):
                at = pl.multiple_of(nc * 1024 + q * 256, 256)
                out_ref[:, pl.ds(at, 256)] = pltpu.matmul_pop(accs[16 + q]).astype(BF)

    pl.run_scoped(
        scoped,
        *[pltpu.ACC(m)((80, 256), F32) for m in range(2) for _ in range(8)],
        *[pltpu.ACC(q % 2)((ROWS, 256), F32) for q in range(4)],
    )


def conv(first, count, nblk, win, half, w, sel, bias, lab, extra, after=()):
    return pl.pallas_call(
        functools.partial(conv_kernel, first, count),
        out_shape=jax.ShapeDtypeStruct((ROWS, count * 1024 + extra), BF),
        in_specs=[pl.BlockSpec(memory_space=pltpu.SMEM)] + [pl.BlockSpec(memory_space=pltpu.VMEM)] * 6
        + [pl.BlockSpec(memory_space=pl.ANY)] * len(after),
        out_specs=pl.BlockSpec(memory_space=pltpu.VMEM),
        scratch_shapes=[pltpu.VMEM((256, 1024), BF)],
        compiler_params=pltpu.CompilerParams(vmem_limit_bytes=40 * 2**20),
        cost_estimate=pl.CostEstimate(flops=count * 2 * 86400 * 256 * 256, bytes_accessed=8 * 2**20, transcendentals=0),
        name="conv",
    )(nblk, win, half, w, sel, bias, lab, *after)


TILES = 16
OWNED = 20
SLOTS = 25
NOTE = 4
FIRST = 5
NTILES = 136
GROUP = 1536
CLASSES = 1000
FEAT = 8


BLOCKS = ((0, 96), (96, 96), (192, 96), (288, 96), (384, 96), (480, 96), (576, 96), (672, 96), (768, 384), (1152, 288), (1440, 96))


def gram_kernel(me_ref, owner_ref, *refs):
    n = len(BLOCKS)
    parts, (out_ref, peak_ref) = (refs[:n], refs[n:2 * n]), refs[2 * n:2 * n + 2]
    fa_ref, fb_ref, ft_ref, target_ref, left_ref, list_i, list_j, sem = refs[2 * n + 2:]
    held = (fa_ref, fb_ref)
    me_tile = me_ref[0, 2]
    copies = [
        [
            pltpu.make_async_copy(ref, held[part].at[start:start + size], sem.at[part * n + k])
            for k, (ref, (start, size)) in enumerate(zip(parts[part], BLOCKS))
        ]
        for part in range(2)
    ]
    for group in copies:
        for copy in group:
            copy.start()

    def scan(k, carry):
        i, j, n = carry
        mine = owner_ref[k] == me_tile

        @pl.when(mine)
        def _():
            list_i[n] = i
            list_j[n] = j

        wrap = j == TILES - 1
        i2 = jnp.where(wrap, i + 1, i)
        return i2, jnp.where(wrap, i2, j + 1), n + mine.astype(jnp.int32)

    _, _, owned = lax.fori_loop(0, NTILES, scan, (jnp.int32(0), jnp.int32(0), jnp.int32(0)))
    peak_ref[...] = jnp.zeros_like(peak_ref)

    @pl.loop(owned, OWNED)
    def _(slot):
        for k in range(FEAT):
            out_ref[k, slot + FIRST] = jnp.zeros((32, 256), F32)

    for part in range(2):
        for copy in copies[part]:
            copy.wait()
        for local in range(2):
            for q in range(4):
                cols = slice(local * 1024 + q * 256, local * 1024 + (q + 1) * 256)
                ft_ref[q * 4 + part * 2 + local] = held[part][:, cols].T
    digit = lax.broadcasted_iota(jnp.int32, (128, 256), 0)
    weight = jnp.where(digit == 0, 8.0, jnp.where(digit == 1, 1.0, 0.0)).astype(BF)
    label = dot(fa_ref[:, 2048:], weight)
    classes = lax.broadcasted_iota(jnp.int32, (GROUP, 256), 1).astype(F32)
    for s in range(4):
        target_ref[:, s * 256:(s + 1) * 256] = jnp.where(label == classes + 256.0 * s, 1.0, -1.0).astype(BF)

    def put(slot, product):
        peak_ref[...] = jnp.maximum(peak_ref[...], jnp.max(jnp.abs(product).reshape(32, 8, 256), axis=0))
        for k in range(FEAT):
            out_ref[k, slot] = product[k * 32:(k + 1) * 32, :]

    start = pl.multiple_of(me_tile % 8 * 32, 32)
    for f in range(FEAT):
        t = f // 2 * 4 + f % 2 * 2 + me_tile // 8
        left_ref[f * 32:(f + 1) * 32, :] = ft_ref[t, pl.ds(start, 32), :]
    for s in range(4):
        put(s, dot(left_ref[...], target_ref[:, s * 256:(s + 1) * 256]))
    for s in range(0, FEAT, 2):
        out_ref[s:s + 2, NOTE] = jnp.zeros((2, 32, 256), F32)

    @pl.loop(0, owned)
    def _(slot):
        j = list_j[slot]
        at = pl.multiple_of(j % 2 * 1024 + j // 4 * 256, 256)
        second = j % 4 >= 2

        @pl.when(second)
        def _():
            put(slot + FIRST, dot(ft_ref[list_i[slot]], fb_ref[:, pl.ds(at, 256)]))

        @pl.when(jnp.logical_not(second))
        def _():
            put(slot + FIRST, dot(ft_ref[list_i[slot]], fa_ref[:, pl.ds(at, 256)]))

    top = jnp.max(jnp.max(peak_ref[...], axis=1, keepdims=True), axis=0, keepdims=True)
    exponent = jnp.floor(jnp.log2(jnp.maximum(jnp.broadcast_to(top, (8, 256)), 1e-30)))
    row = lax.broadcasted_iota(jnp.int32, (8, 256), 0)
    peak_ref[...] = jnp.where(row == 0, exponent, jnp.exp2(13.0 - exponent))


def gram(me, tile_owner, parts):
    smem = pl.BlockSpec(memory_space=pltpu.SMEM)
    vmem = pl.BlockSpec(memory_space=pltpu.VMEM)
    return pl.pallas_call(
        gram_kernel,
        out_shape=(jax.ShapeDtypeStruct((FEAT, SLOTS, 32, 256), F32), jax.ShapeDtypeStruct((8, 256), F32)),
        in_specs=[smem, smem] + [pl.BlockSpec(memory_space=pltpu.HBM)] * (2 * len(BLOCKS)),
        out_specs=(vmem, vmem),
        scratch_shapes=[
            pltpu.VMEM((GROUP, 2176), BF),
            pltpu.VMEM((GROUP, 2048), BF),
            pltpu.VMEM((TILES, 256, GROUP), BF),
            pltpu.VMEM((GROUP, 1024), BF),
            pltpu.VMEM((256, GROUP), BF),
            pltpu.SMEM((OWNED,), jnp.int32),
            pltpu.SMEM((OWNED,), jnp.int32),
            pltpu.SemaphoreType.DMA((2 * len(BLOCKS),)),
        ],
        compiler_params=pltpu.CompilerParams(vmem_limit_bytes=40 * 2**20),
        cost_estimate=pl.CostEstimate(flops=5 * 10**9, bytes_accessed=20 * 2**20, transcendentals=0),
        name="gram",
    )(me, tile_owner, *parts[0], *parts[1])


HALF = jnp.float16


STEPS = (8, 12, 20)


def exchange(partial, peak, owned):
    exponent = peak[0].reshape(1, 1, 1, 256)
    scale = peak[1].reshape(1, 1, 1, 256)

    def some(count, partial):
        used = partial[:, :FIRST + count]
        note = lax.broadcasted_iota(jnp.int32, used.shape, 1) == NOTE
        coded = jnp.where(note, exponent, used * scale).astype(HALF)
        got = lax.all_to_all(coded, "feat", split_axis=0, concat_axis=0, tiled=True)
        back = jnp.exp2(got[:, NOTE:FIRST, :1, :1].astype(F32) - 13.0) * (1.0 / 12288.0)
        total = jnp.sum(got.astype(F32) * back, axis=0)
        cross = total[:NOTE].transpose(1, 0, 2).reshape(32, 1024)[:, :CLASSES]
        return jnp.pad(total[FIRST:], ((0, OWNED - count), (0, 0), (0, 0))), cross

    level = sum((owned > step).astype(jnp.int32) for step in STEPS[:-1])
    return lax.switch(level, [functools.partial(some, step) for step in STEPS], partial)


def hop(dy=0, dx=0, core=0):
    def index(y, x, c):
        return (y % 2 * 4 + x % 4) * 2 + c % 2

    return [(index(y, x, c), index(y + dy, x + dx, c + core)) for y in range(2) for x in range(4) for c in range(2)]


def onward():
    return [(s, d) if s % 2 == 0 else (s, e) for (s, d), (_, e) in zip(hop(dx=1), hop(dx=-1))]


def send(block, perm):
    return lax.ppermute(block, "tile", perm)


def spread_first(own):
    left = send(own, hop(dx=1))
    right = send(own, hop(dx=-1))
    over = send(own, hop(dy=1))
    return own, over, left, right


def spread_second(first):
    own, over, left, right = first
    even = lax.axis_index("tile") % 2 == 0
    far = send(jnp.where(even, left, right), onward())
    over_left = send(over, hop(dx=1))
    over_right = send(over, hop(dx=-1))
    swap_a = send(jnp.concatenate([own, over, left, right], axis=0), hop(core=1))
    return far, over_left, over_right, swap_a


def spread_third(first, second):
    own, over, left, right = first
    far, over_left, over_right, swap_a = second
    even = lax.axis_index("tile") % 2 == 0
    over_far = send(jnp.where(even, over_left, over_right), onward())
    swap_b = send(jnp.concatenate([over_left, over_right, far], axis=0), hop(core=1))
    swap_c = send(over_far, hop(core=1))
    return [own, over, left, right, over_left, over_right, far, over_far, swap_a, swap_b, swap_c]


def body(images, row_list, labels, filters, bias, tile_owner):
    me = lax.axis_index("tile").astype(jnp.int32).reshape(1)
    win, half, w, sel, lab, nblk = prep(me, tile_owner, images, row_list, labels, filters)
    bias4 = bias.reshape(4, 1, 256)
    own_a = conv(0, 2, nblk, win, half, w, sel, bias4, lab, 128)
    first_a = spread_first(own_a)
    own_b2 = conv(2, 1, nblk, win, half, w, sel, bias4, lab, 0, (own_a,))
    second_a = spread_second(first_a)
    own_b3 = conv(3, 1, nblk, win, half, w, sel, bias4, lab, 0, first_a[1:])
    own_b = jnp.concatenate([own_b2, own_b3], axis=1)
    own_b, far, over_left, over_right = lax.optimization_barrier((own_b,) + second_a[:3])
    second_a = (far, over_left, over_right, second_a[3])
    first_b = spread_first(own_b)
    part_a = spread_third(first_a, second_a)
    second_b = spread_second(first_b)
    part_b = spread_third(first_b, second_b)
    partial, peak = gram(nblk, tile_owner, (part_a, part_b))
    return exchange(partial, peak, nblk[0, 3])


def solution(mesh):
    def run(*args):
        return jax.shard_map(
            body,
            mesh=mesh,
            in_specs=(P(("feat", "tile"), None), P(("feat", "tile")), P(("feat", "tile")), P(), P(), P()),
            out_specs=(P("tile", "feat", None), P(("feat", "tile"), None)),
            check_vma=False,
        )(*args)

    return run
```

```python
import functools

import jax
import jax.numpy as jnp
from jax import lax
from jax.experimental import pallas as pl
from jax.experimental.pallas import tpu as pltpu
from jax.sharding import PartitionSpec as P

ROWS = 96
BLK = 16
NBLK = 6
WIDE = 112
BF = jnp.bfloat16
F32 = jnp.float32
LAG = 3


def dot(a, b, dims=(((1,), (0,)), ((), ()))):
    return lax.dot_general(a, b, dims, preferred_element_type=F32)


def prep_kernel(me_ref, owner_ref, rows_ref, labels_ref, filt_ref, img_hbm, win_ref, half_ref, w_ref, sel_ref, lab_ref, nblk_ref, img_ref, x_ref, pick_ref, flat_ref, sem):
    fetch = pltpu.make_async_copy(img_hbm, img_ref, sem)
    fetch.start()
    flat_ref[...] = jnp.zeros_like(flat_ref)
    for i in range(6):
        for j in range(6):
            p = 6 * i + j
            flat_ref[3 * p:3 * p + 3, :] = filt_ref[i, j].astype(F32)
    rows_i = lax.broadcasted_iota(jnp.int32, (1536, 128), 0)
    cols_i = lax.broadcasted_iota(jnp.int32, (1536, 128), 1)
    d = rows_i // 256
    di = d // 3
    dj = d - 3 * di
    r = rows_i % 256 // 32 - 2 * di
    c = rows_i % 32 - 6 * dj
    ok = (r >= 0) & (r < 6) & (c >= 0) & (c < 18)
    spread = jnp.where(ok & (cols_i == r * 18 + c), 1.0, 0.0).astype(BF)
    for nc in range(4):
        w_ref[nc] = dot(spread, flat_ref[:, nc * 256:(nc + 1) * 256].astype(BF)).astype(BF)

    lanes = lax.broadcasted_iota(jnp.int32, (ROWS, 128), 1)
    subs = lax.broadcasted_iota(jnp.int32, (ROWS, 128), 0)
    rows = jnp.broadcast_to(rows_ref[...], (128, 128)).astype(F32).T[:ROWS]
    hit = rows.astype(jnp.int32) == lanes
    used = jnp.max(jnp.where(hit, 1.0, 0.0), axis=0, keepdims=True)
    low = lax.broadcasted_iota(jnp.int32, (128, 128), 0)
    high = lax.broadcasted_iota(jnp.int32, (128, 128), 1)
    upto = jnp.where(low <= high, 1.0, 0.0).astype(BF)
    rank = dot(jnp.broadcast_to(used, (16, 128)).astype(BF), upto)[0:1] - 1.0
    rank = rank.astype(jnp.int32)
    total = jnp.sum(used).astype(jnp.int32)
    whole = (total + 7) // BLK
    nblk_ref[0, 0] = whole
    nblk_ref[0, 1] = total - whole * BLK
    nblk_ref[0, 2] = me_ref[0]
    nblk_ref[0, 3] = jnp.sum(jnp.where(owner_ref[...] == me_ref[0], 1.0, 0.0)).astype(jnp.int32)
    deep = lax.broadcasted_iota(jnp.int32, (WIDE, 128), 0)
    deep = jnp.where(deep < ROWS, deep, jnp.where(deep < ROWS + 8, deep - ROWS + BLK * whole, -1))
    take = jnp.where((deep == rank) & (used > 0.0), 1.0, 0.0).astype(BF)
    compact = take[:ROWS]
    sel_ref[:, :ROWS] = dot(jnp.where(hit, 1.0, 0.0).astype(BF), compact, (((1,), (1,)), ((), ()))).astype(BF)
    sel_ref[:, ROWS:] = jnp.zeros((ROWS, 256 - ROWS), BF)
    label = jnp.sum(jnp.where(hit, labels_ref[...], 0), axis=1, keepdims=True)
    coarse = label // 8
    fine = label - coarse * 8
    lab_ref[...] = jnp.where(lanes == 0, coarse, jnp.where(lanes == 1, fine, 0)).astype(BF)
    col = lax.broadcasted_iota(jnp.int32, (1, 1280), 1)
    within = col % 32
    source = (col % 128) // 32 * 192 + 18 * (col // 128) + within
    source = jnp.where(within < 30, source, -1)
    place = lax.broadcasted_iota(jnp.int32, (768, 1280), 0)
    pick_ref[...] = jnp.where(place == source, 1.0, 0.0).astype(BF)
    fetch.wait()
    for part in range(16):
        x_ref[part * WIDE:(part + 1) * WIDE, :] = dot(take[:, :ROWS], img_ref[:, part * 768:(part + 1) * 768]).astype(BF)

    @pl.loop(0, 5)
    def _(n):
        fine = dot(x_ref[...], pick_ref[:, pl.ds(pl.multiple_of(n * 256, 256), 256)])
        tile = fine.astype(BF)
        for part in range(16):
            row = part * WIDE + ROWS
            pair = jnp.concatenate([fine[row:row + 8, :128], fine[row:row + 8, 128:]], axis=0)
            half_ref[part, pl.ds(pl.multiple_of(n * 16, 16), 16), :] = pair.astype(BF)
        for h in range(2):
            at = pl.multiple_of((2 * n + h) * 16, 16)
            for part in range(16):
                for b in range(NBLK):
                    row = part * WIDE + b * 16
                    win_ref[part, b, pl.ds(at, 16), :] = tile[row:row + 16, h * 128:(h + 1) * 128]


def prep(me, tile_owner, images, row_list, labels, filters):
    vmem = pl.BlockSpec(memory_space=pltpu.VMEM)
    return pl.pallas_call(
        prep_kernel,
        out_shape=(
            jax.ShapeDtypeStruct((16, NBLK, 160, 128), BF),
            jax.ShapeDtypeStruct((16, 80, 128), BF),
            jax.ShapeDtypeStruct((4, 1536, 256), BF),
            jax.ShapeDtypeStruct((ROWS, 256), BF),
            jax.ShapeDtypeStruct((ROWS, 128), BF),
            jax.ShapeDtypeStruct((1, 4), jnp.int32),
        ),
        in_specs=[pl.BlockSpec(memory_space=pltpu.SMEM), vmem, vmem, vmem, vmem, pl.BlockSpec(memory_space=pl.ANY)],
        out_specs=(vmem, vmem, vmem, vmem, vmem, pl.BlockSpec(memory_space=pltpu.SMEM)),
        scratch_shapes=[
            pltpu.VMEM((ROWS, 12288), BF),
            pltpu.VMEM((16 * WIDE, 768), BF),
            pltpu.VMEM((768, 1280), BF),
            pltpu.VMEM((128, 1024), F32),
            pltpu.SemaphoreType.DMA,
        ],
        compiler_params=pltpu.CompilerParams(vmem_limit_bytes=40 * 2**20),
        name="prep",
    )(me, tile_owner.reshape(1, NTILES), jnp.pad(row_list, (0, 32)).reshape(1, 128), jnp.pad(labels, (0, 32)).reshape(1, 128), filters, images)


def conv_kernel(first, count, nblk_ref, win_ref, half_ref, w_ref, sel_ref, bias_ref, lab_ref, *refs):
    out_ref, uniq_ref = refs[-2:]
    uniq_ref[...] = jnp.zeros_like(uniq_ref)
    if out_ref.shape[1] > count * 1024:
        out_ref[:, count * 1024:] = lab_ref[...]
    steps = []
    for d in range(6):
        for w in range(15):
            steps.append((d, w, 0 if w <= (7 if d < 3 else 6) else 1))

    def block(nc, b, bias, floor, acc):
        total = [[jnp.zeros((16, 256), F32) for _ in range(2)] for _ in range(2)]

        def take(k):
            qr = steps[k][2]
            for m in range(2):
                got = pltpu.matmul_pop(acc[m][k % 8]).reshape(5, 16, 256)
                total[qr][m] = total[qr][m] + jnp.sum(jnp.maximum(got, floor[None]), axis=0)

        for k, (d, w, _) in enumerate(steps):
            if w == 0:
                for m in range(2):
                    pltpu.matmul_push_rhs(w_ref[first + nc, d * 256:(d + 1) * 256, :], d % 2, m)
            for m in range(2):
                rows = slice(m * 80, (m + 1) * 80)
                lhs = jnp.concatenate([win_ref[w, b, rows, :], win_ref[w + 1, b, rows, :]], axis=1)
                pltpu.matmul_acc_lhs(acc[m][k % 8], lhs, load_staged_rhs=d % 2 if w == 0 else None)
            if k >= LAG:
                take(k - LAG)
        for k in range(len(steps) - LAG, len(steps)):
            take(k)
        at = pl.multiple_of(b * 16, 16)
        for qr in range(2):
            for m in range(2):
                q = 2 * qr + m
                mean = (total[qr][m] + 225.0 * bias) * (1.0 / 225.0)
                uniq_ref[pl.ds(at, 16), q * 256:(q + 1) * 256] = mean.astype(BF)

    def half_block(nc, b, bias, floor, acc):
        total = [[jnp.zeros((8, 256), F32) for _ in range(2)] for _ in range(2)]
        low = floor[:8]

        def take(k):
            d, j = k // 8, k % 8
            for m in range(2):
                w = 2 * j + m
                if w < 15:
                    qr = 0 if w <= (7 if d < 3 else 6) else 1
                    got = jnp.maximum(pltpu.matmul_pop(acc[m][k % 8]).reshape(10, 8, 256), low[None])
                    total[qr][0] = total[qr][0] + jnp.sum(got[:5], axis=0)
                    total[qr][1] = total[qr][1] + jnp.sum(got[5:], axis=0)

        for k in range(48):
            d, j = k // 8, k % 8
            if j == 0:
                for m in range(2):
                    pltpu.matmul_push_rhs(w_ref[first + nc, d * 256:(d + 1) * 256, :], d % 2, m)
            for m in range(2):
                w = 2 * j + m
                if w < 15:
                    lhs = jnp.concatenate([half_ref[w], half_ref[w + 1]], axis=1)
                    pltpu.matmul_acc_lhs(acc[m][k % 8], lhs, load_staged_rhs=d % 2 if j == 0 else None)
            if k >= LAG:
                take(k - LAG)
        for k in range(48 - LAG, 48):
            take(k)
        at = pl.multiple_of(b * 16, 16)
        for q in range(4):
            mean = (total[q // 2][q % 2] + 225.0 * bias) * (1.0 / 225.0)
            uniq_ref[pl.ds(at, 16), q * 256:(q + 1) * 256] = jnp.concatenate([mean, jnp.zeros_like(mean)], axis=0).astype(BF)

    def scoped(*accs):
        @pl.loop(0, count)
        def _(nc):
            bias = bias_ref[first + nc]
            floor = jnp.broadcast_to(-bias, (16, 256))

            @pl.loop(0, nblk_ref[0, 0])
            def _(b):
                block(nc, b, bias, floor, (accs[:8], accs[8:16]))

            @pl.when(nblk_ref[0, 1] > 0)
            def _():
                half_block(nc, nblk_ref[0, 0], bias, floor, (accs[:8], accs[8:16]))

            for m in range(2):
                for qr in range(2):
                    q = 2 * qr + m
                    pltpu.matmul_push_rhs(uniq_ref[:, q * 256:(q + 1) * 256], qr, m)
                    pltpu.matmul_acc_lhs(accs[16 + q], sel_ref[...], load_staged_rhs=qr)
            for q in range(4):
                at = pl.multiple_of(nc * 1024 + q * 256, 256)
                out_ref[:, pl.ds(at, 256)] = pltpu.matmul_pop(accs[16 + q]).astype(BF)

    pl.run_scoped(
        scoped,
        *[pltpu.ACC(m)((80, 256), F32) for m in range(2) for _ in range(8)],
        *[pltpu.ACC(q % 2)((ROWS, 256), F32) for q in range(4)],
    )


def conv(first, count, nblk, win, half, w, sel, bias, lab, extra, after=()):
    return pl.pallas_call(
        functools.partial(conv_kernel, first, count),
        out_shape=jax.ShapeDtypeStruct((ROWS, count * 1024 + extra), BF),
        in_specs=[pl.BlockSpec(memory_space=pltpu.SMEM)] + [pl.BlockSpec(memory_space=pltpu.VMEM)] * 6
        + [pl.BlockSpec(memory_space=pl.ANY)] * len(after),
        out_specs=pl.BlockSpec(memory_space=pltpu.VMEM),
        scratch_shapes=[pltpu.VMEM((256, 1024), BF)],
        compiler_params=pltpu.CompilerParams(vmem_limit_bytes=40 * 2**20),
        cost_estimate=pl.CostEstimate(flops=count * 2 * 86400 * 256 * 256, bytes_accessed=8 * 2**20, transcendentals=0),
        name="conv",
    )(nblk, win, half, w, sel, bias, lab, *after)


TILES = 16
OWNED = 20
SLOTS = 25
NOTE = 4
FIRST = 5
NTILES = 136
GROUP = 1536
CLASSES = 1000
FEAT = 8


BLOCKS = ((0, 96), (96, 96), (192, 96), (288, 96), (384, 96), (480, 96), (576, 96), (672, 96), (768, 384), (1152, 288), (1440, 96))


def gram_kernel(me_ref, owner_ref, *refs):
    n = len(BLOCKS)
    parts, (out_ref, peak_ref) = (refs[:n], refs[n:2 * n]), refs[2 * n:2 * n + 2]
    fa_ref, fb_ref, ft_ref, target_ref, left_ref, list_i, list_j, sem = refs[2 * n + 2:]
    held = (fa_ref, fb_ref)
    me_tile = me_ref[0, 2]
    copies = [
        [
            pltpu.make_async_copy(ref, held[part].at[start:start + size], sem.at[part * n + k])
            for k, (ref, (start, size)) in enumerate(zip(parts[part], BLOCKS))
        ]
        for part in range(2)
    ]
    for group in copies:
        for copy in group:
            copy.start()

    def scan(k, carry):
        i, j, n = carry
        mine = owner_ref[k] == me_tile

        @pl.when(mine)
        def _():
            list_i[n] = i
            list_j[n] = j

        wrap = j == TILES - 1
        i2 = jnp.where(wrap, i + 1, i)
        return i2, jnp.where(wrap, i2, j + 1), n + mine.astype(jnp.int32)

    _, _, owned = lax.fori_loop(0, NTILES, scan, (jnp.int32(0), jnp.int32(0), jnp.int32(0)))
    peak_ref[...] = jnp.zeros_like(peak_ref)

    @pl.loop(owned, OWNED)
    def _(slot):
        for k in range(FEAT):
            out_ref[k, slot + FIRST] = jnp.zeros((32, 256), F32)

    for part in range(2):
        for copy in copies[part]:
            copy.wait()
        for local in range(2):
            for q in range(4):
                cols = slice(local * 1024 + q * 256, local * 1024 + (q + 1) * 256)
                ft_ref[q * 4 + part * 2 + local] = held[part][:, cols].T
    digit = lax.broadcasted_iota(jnp.int32, (128, 256), 0)
    weight = jnp.where(digit == 0, 8.0, jnp.where(digit == 1, 1.0, 0.0)).astype(BF)
    label = dot(fa_ref[:, 2048:], weight)
    classes = lax.broadcasted_iota(jnp.int32, (GROUP, 256), 1).astype(F32)
    for s in range(4):
        target_ref[:, s * 256:(s + 1) * 256] = jnp.where(label == classes + 256.0 * s, 1.0, -1.0).astype(BF)

    def put(slot, product):
        peak_ref[...] = jnp.maximum(peak_ref[...], jnp.max(jnp.abs(product).reshape(32, 8, 256), axis=0))
        for k in range(FEAT):
            out_ref[k, slot] = product[k * 32:(k + 1) * 32, :]

    start = pl.multiple_of(me_tile % 8 * 32, 32)
    for f in range(FEAT):
        t = f // 2 * 4 + f % 2 * 2 + me_tile // 8
        left_ref[f * 32:(f + 1) * 32, :] = ft_ref[t, pl.ds(start, 32), :]
    for s in range(4):
        put(s, dot(left_ref[...], target_ref[:, s * 256:(s + 1) * 256]))
    for s in range(0, FEAT, 2):
        out_ref[s:s + 2, NOTE] = jnp.zeros((2, 32, 256), F32)

    @pl.loop(0, owned)
    def _(slot):
        j = list_j[slot]
        at = pl.multiple_of(j % 2 * 1024 + j // 4 * 256, 256)
        second = j % 4 >= 2

        @pl.when(second)
        def _():
            put(slot + FIRST, dot(ft_ref[list_i[slot]], fb_ref[:, pl.ds(at, 256)]))

        @pl.when(jnp.logical_not(second))
        def _():
            put(slot + FIRST, dot(ft_ref[list_i[slot]], fa_ref[:, pl.ds(at, 256)]))

    top = jnp.max(jnp.max(peak_ref[...], axis=1, keepdims=True), axis=0, keepdims=True)
    exponent = jnp.floor(jnp.log2(jnp.maximum(jnp.broadcast_to(top, (8, 256)), 1e-30)))
    row = lax.broadcasted_iota(jnp.int32, (8, 256), 0)
    peak_ref[...] = jnp.where(row == 0, exponent, jnp.exp2(13.0 - exponent))


def gram(me, tile_owner, parts):
    smem = pl.BlockSpec(memory_space=pltpu.SMEM)
    vmem = pl.BlockSpec(memory_space=pltpu.VMEM)
    return pl.pallas_call(
        gram_kernel,
        out_shape=(jax.ShapeDtypeStruct((FEAT, SLOTS, 32, 256), F32), jax.ShapeDtypeStruct((8, 256), F32)),
        in_specs=[smem, smem] + [pl.BlockSpec(memory_space=pltpu.HBM)] * (2 * len(BLOCKS)),
        out_specs=(vmem, vmem),
        scratch_shapes=[
            pltpu.VMEM((GROUP, 2176), BF),
            pltpu.VMEM((GROUP, 2048), BF),
            pltpu.VMEM((TILES, 256, GROUP), BF),
            pltpu.VMEM((GROUP, 1024), BF),
            pltpu.VMEM((256, GROUP), BF),
            pltpu.SMEM((OWNED,), jnp.int32),
            pltpu.SMEM((OWNED,), jnp.int32),
            pltpu.SemaphoreType.DMA((2 * len(BLOCKS),)),
        ],
        compiler_params=pltpu.CompilerParams(vmem_limit_bytes=56 * 2**20),
        cost_estimate=pl.CostEstimate(flops=5 * 10**9, bytes_accessed=20 * 2**20, transcendentals=0),
        name="gram",
    )(me, tile_owner, *parts[0], *parts[1])


HALF = jnp.float16


STEPS = (8, 12, 20)


def exchange(partial, peak, owned):
    exponent = peak[0].reshape(1, 1, 1, 256)
    scale = peak[1].reshape(1, 1, 1, 256)

    def some(count, partial):
        used = partial[:, :FIRST + count]
        note = lax.broadcasted_iota(jnp.int32, used.shape, 1) == NOTE
        coded = jnp.where(note, exponent, used * scale).astype(HALF)
        got = lax.all_to_all(coded, "feat", split_axis=0, concat_axis=0, tiled=True)
        back = jnp.exp2(got[:, NOTE:FIRST, :1, :1].astype(F32) - 13.0) * (1.0 / 12288.0)
        total = jnp.sum(got.astype(F32) * back, axis=0)
        cross = total[:NOTE].transpose(1, 0, 2).reshape(32, 1024)[:, :CLASSES]
        return jnp.pad(total[FIRST:], ((0, OWNED - count), (0, 0), (0, 0))), cross

    level = sum((owned > step).astype(jnp.int32) for step in STEPS[:-1])
    return lax.switch(level, [functools.partial(some, step) for step in STEPS], partial)


def hop(dy=0, dx=0, core=0):
    def index(y, x, c):
        return (y % 2 * 4 + x % 4) * 2 + c % 2

    return [(index(y, x, c), index(y + dy, x + dx, c + core)) for y in range(2) for x in range(4) for c in range(2)]


def onward():
    return [(s, d) if s % 2 == 0 else (s, e) for (s, d), (_, e) in zip(hop(dx=1), hop(dx=-1))]


def send(block, perm):
    return lax.ppermute(block, "tile", perm)


def spread_first(own):
    left = send(own, hop(dx=1))
    right = send(own, hop(dx=-1))
    over = send(own, hop(dy=1))
    return own, over, left, right


def spread_second(first):
    own, over, left, right = first
    even = lax.axis_index("tile") % 2 == 0
    far = send(jnp.where(even, left, right), onward())
    over_left = send(over, hop(dx=1))
    over_right = send(over, hop(dx=-1))
    swap_a = send(jnp.concatenate([own, over, left, right], axis=0), hop(core=1))
    return far, over_left, over_right, swap_a


def spread_third(first, second):
    own, over, left, right = first
    far, over_left, over_right, swap_a = second
    even = lax.axis_index("tile") % 2 == 0
    over_far = send(jnp.where(even, over_left, over_right), onward())
    swap_b = send(jnp.concatenate([over_left, over_right, far], axis=0), hop(core=1))
    swap_c = send(over_far, hop(core=1))
    return [own, over, left, right, over_left, over_right, far, over_far, swap_a, swap_b, swap_c]


def body(images, row_list, labels, filters, bias, tile_owner):
    me = lax.axis_index("tile").astype(jnp.int32).reshape(1)
    win, half, w, sel, lab, nblk = prep(me, tile_owner, images, row_list, labels, filters)
    bias4 = bias.reshape(4, 1, 256)
    own_a = conv(0, 2, nblk, win, half, w, sel, bias4, lab, 128)
    first_a = spread_first(own_a)
    own_b2 = conv(2, 1, nblk, win, half, w, sel, bias4, lab, 0, (own_a,))
    second_a = spread_second(first_a)
    own_b3 = conv(3, 1, nblk, win, half, w, sel, bias4, lab, 0, first_a[1:])
    own_b = jnp.concatenate([own_b2, own_b3], axis=1)
    own_b, far, over_left, over_right = lax.optimization_barrier((own_b,) + second_a[:3])
    second_a = (far, over_left, over_right, second_a[3])
    first_b = spread_first(own_b)
    part_a = spread_third(first_a, second_a)
    second_b = spread_second(first_b)
    part_b = spread_third(first_b, second_b)
    partial, peak = gram(nblk, tile_owner, (part_a, part_b))
    return exchange(partial, peak, nblk[0, 3])


def solution(mesh):
    def run(*args):
        return jax.shard_map(
            body,
            mesh=mesh,
            in_specs=(P(("feat", "tile"), None), P(("feat", "tile")), P(("feat", "tile")), P(), P(), P()),
            out_specs=(P("tile", "feat", None), P(("feat", "tile"), None)),
            check_vma=False,
        )(*args)

    return run
```
